256 devices in a mesh: ctx: 64 (over y, z, core), dp: 4 (over x).
Axes of the slice: x: 4, y: 4, z: 8, core: 2. Of those that a mesh axis runs over, the one named last changes fastest.
Arguments:
- tokens: bfloat16 [4, 16384, 4096], P('dp', 'ctx'), may hold values from -16 to 16
- projected: bfloat16 [4, 16384, 6144], P('dp', 'ctx'), may hold values from -6 to 6
- down_proj: bfloat16 [3, 4096, 32], replicated, may hold values from -0.09375 to 0.09375
- up_projection: bfloat16 [3, 32, 2048], replicated, may hold values from -1 to 1
- block_ids: int32 [4, 64, 3], P('dp'), may hold values from 0 to 63, as said below
- cotangent: bfloat16 [4, 16384, 2048], P('dp', 'ctx'), may hold values from -192 to 192
Outputs:
- attn_out: bfloat16 [4, 16384, 2048], P('dp', 'ctx')
- grad_proj: bfloat16 [4, 16384, 6144], P('dp', 'ctx')
- grad_down: float32 [3, 4096, 32], P(None, ('ctx', 'dp'))
- grad_up: float32 [3, 32, 2048], P(None, None, ('ctx', 'dp'))
The draws below stay inside these ranges and needn't reach their ends.
Inputs may be any that keep to these rules, and one draw needn't show every extreme that they name: block_ids[r, b, 0] = b. Slots 1 and 2 name two different blocks below b, or b itself where the slot is empty (both empty for b = 0, slot 2 for b = 1). In each replica no block is named in the other slots of more than 6 query blocks, and some block is named by exactly 6.
All inputs are finite; a program needn't handle non-finite values.
Results may differ from the reference program's by a relative error of at most 0.012.
The reference program's roundings to bfloat16 on the way count: a program that leaves them out, or rounds other values in their place, can miss the bound.
Values may be sent and summed in bfloat16 or wider, within the bound.
No kernel may reach another device: no remote copies, remote signals or barrier semaphores. Data moves between devices by JAX's collectives and lax.ppermute only.
A program may use at most 192 MiB of HBM per device.

```python
import jax
import jax.numpy as jnp
from jax import lax

D = 4096
H = 16
HD = 128
R = 32
BLK = 256
TOPK = 3
MOST = 6
KEY_VALUE_BLOCKS = 64
REPLICAS = 4
TOKENS = 16384
HQ = 2048
N_DP = 4


def draw_tokens(key, part):
    key = jax.random.fold_in(key, 23)
    base_key, pair_key = jax.random.split(key, 2)
    values = jnp.clip(jax.random.normal(base_key, (REPLICAS, TOKENS, D), jnp.float32), -3.5, 3.5)
    pairing = jax.random.permutation(pair_key, REPLICAS * KEY_VALUE_BLOCKS).reshape(REPLICAS, KEY_VALUE_BLOCKS)
    target = pairing[:, jnp.arange(TOKENS) // BLK]
    column_block = jnp.arange(D) // (D // (REPLICAS * KEY_VALUE_BLOCKS))
    values = values * jnp.where(column_block[None, None, :] == target[:, :, None], 3.0, 1.0)
    return values.astype(jnp.bfloat16)


def draw_projected(key, part):
    key = jax.random.fold_in(key, 11)
    base_key = jax.random.fold_in(key, 0)
    values = jnp.clip(jax.random.normal(base_key, (REPLICAS, KEY_VALUE_BLOCKS, BLK, 3, HQ), jnp.float32), -5.0, 5.0)
    return values.reshape(REPLICAS, TOKENS, 3 * HQ).astype(jnp.bfloat16)


def pick_blocks(key):
    first_key, order_key, noise_key = jax.random.split(key, 3)
    leading_block = jax.random.randint(first_key, (), 0, KEY_VALUE_BLOCKS // 4)
    ordering = jax.random.permutation(order_key, KEY_VALUE_BLOCKS)
    popular_blocks = jnp.zeros((KEY_VALUE_BLOCKS,), jnp.int32).at[ordering[:max(1, KEY_VALUE_BLOCKS // 16)]].set(4096)
    extra_score = jnp.where(jnp.arange(KEY_VALUE_BLOCKS) == leading_block, 8192, popular_blocks)
    random_offset = jax.random.randint(noise_key, (KEY_VALUE_BLOCKS, KEY_VALUE_BLOCKS), 0, 1024)
    candidate_block = jnp.arange(KEY_VALUE_BLOCKS, dtype=jnp.int32)

    def step(loads, current_block):
        block_ranking = (extra_score + random_offset[current_block]) * KEY_VALUE_BLOCKS + (KEY_VALUE_BLOCKS - 1 - candidate_block)
        allowed = (candidate_block < current_block) & (loads < MOST)
        block_ranking = jnp.where(allowed, block_ranking, -1)
        best, position = lax.top_k(block_ranking, 2)
        slots = jnp.where(best >= 0, position, current_block).astype(jnp.int32)
        taken = (candidate_block[None, :] == slots[:, None]) & (best[:, None] >= 0)
        loads = loads + jnp.sum(taken.astype(jnp.int32), axis=0)
        return (loads, jnp.concatenate([current_block[None], slots]))
    _, chosen = lax.scan(step, jnp.zeros((KEY_VALUE_BLOCKS,), jnp.int32), jnp.arange(KEY_VALUE_BLOCKS, dtype=jnp.int32))
    return chosen


def draw_block_ids(key, part):
    key = jax.random.fold_in(key, 7)
    return jax.vmap(lambda replica: pick_blocks(jax.random.fold_in(key, replica)))(jnp.arange(REPLICAS))


def steps_of(stream_key, dims, cuts, low, high):
    def one(dim, blocks):
        draws = jax.random.uniform(jax.random.fold_in(jax.random.fold_in(stream_key, 6), dim), (blocks,), jnp.float32, low / len(cuts), high / len(cuts))
        return jnp.repeat(jnp.exp(draws), dims[dim] // blocks).reshape((-1,) + (1,) * (len(dims) - dim - 1))

    factor_of = one(*cuts[0])
    for cut in cuts[1:]:
        factor_of = factor_of * one(*cut)
    return factor_of


def normal_values(own_key, extent, deviation, most, cuts=(), kind=jnp.bfloat16):
    result = jax.random.normal(own_key, extent, jnp.float32) * deviation
    if len(cuts) > 0:
        result = steps_of(own_key, extent, cuts, -0.22, 0.18) * result
    return jnp.clip(result, min=-most, max=most).astype(kind)


def setup_inputs(seed: int = 0) -> dict:
    splits = jax.random.split(jax.random.key(seed), 7)
    tokens = draw_tokens(jax.random.fold_in(splits[6], 71), 0)
    projected = draw_projected(jax.random.fold_in(splits[6], 71), 0)
    down_proj = normal_values(splits[2], (3, D, R), D ** -0.5, 0.09375)
    up_projection = normal_values(splits[3], (3, R, HQ), R ** -0.5, 1.0)
    block_ids = draw_block_ids(jax.random.fold_in(splits[6], 71), 0)
    cotangent = normal_values(splits[5], (REPLICAS, TOKENS, HQ), 32.0, 192.0, ((0, 4), (1, 64)))
    return {"tokens": tokens, "projected": projected, "down_proj": down_proj, "up_projection": up_projection, "block_ids": block_ids, "cotangent": cotangent}


adapter_scale = 0.5


def with_adapters(inputs, frozen_proj, down_proj, up_projection):
    low_rank_states = []
    field_list = []
    for group_member in range(3):
        low_rank = jnp.dot(inputs, down_proj[group_member], preferred_element_type=jnp.float32).astype(jnp.bfloat16)
        adapter_result = jnp.dot(low_rank, up_projection[group_member], preferred_element_type=jnp.float32)
        frozen_weight = frozen_proj[:, group_member * HQ:(group_member + 1) * HQ].astype(jnp.float32)
        field_list.append((frozen_weight + adapter_scale * adapter_result).astype(jnp.bfloat16))
        low_rank_states.append(low_rank)
    return low_rank_states, field_list


def block_pass(queries, key_rows, value_rows, grad_rows, usable):
    score_scale = HD ** -0.5
    key_count = TOPK * BLK
    query_f = queries.astype(jnp.float32).reshape(BLK, H, HD)
    key_f = key_rows.astype(jnp.float32).reshape(key_count, H, HD)
    value_f = value_rows.astype(jnp.float32).reshape(key_count, H, HD)
    grad_f = grad_rows.astype(jnp.float32).reshape(BLK, H, HD)
    key_slot = jnp.arange(key_count, dtype=jnp.int32) // BLK
    causal = (jnp.arange(key_count, dtype=jnp.int32) % BLK)[None, :] <= jnp.arange(BLK, dtype=jnp.int32)[:, None]
    slot_open = jnp.any((key_slot[:, None] == jnp.arange(TOPK, dtype=jnp.int32)[None, :]) & usable[None, :], axis=1)
    visible = jnp.where((key_slot == 0)[None, :], causal, slot_open[None, :])
    scores = jnp.einsum('qhd,khd->hqk', query_f, key_f) * score_scale
    scores = jnp.where(visible[None], scores, -jnp.inf)
    shifted = jnp.exp(scores - jnp.max(scores, axis=-1, keepdims=True))
    attn_probs = shifted / jnp.sum(shifted, axis=-1, keepdims=True)
    weights = attn_probs.astype(jnp.bfloat16)
    attended = jnp.einsum('hqk,khd->qhd', weights.astype(jnp.float32), value_f).astype(jnp.bfloat16)
    drift = jnp.sum(attended.astype(jnp.float32) * grad_f, axis=-1)
    dprobs = jnp.einsum('qhd,khd->hqk', grad_f, value_f)
    dscores = (attn_probs * (dprobs - jnp.transpose(drift)[:, :, None]) * score_scale).astype(jnp.bfloat16)
    dscore_f = dscores.astype(jnp.float32)
    dquery = jnp.einsum('hqk,khd->qhd', dscore_f, key_f).reshape(BLK, HQ)
    dkey = jnp.einsum('hqk,qhd->khd', dscore_f, query_f).reshape(key_count, HQ)
    dvalue = jnp.einsum('hqk,qhd->khd', weights.astype(jnp.float32), grad_f).reshape(key_count, HQ)
    return attended.reshape(BLK, HQ), dquery, jnp.concatenate([dkey, dvalue], axis=1)


def one_replica(inputs, frozen_proj, down_proj, up_projection, chosen, grad_out):
    low_rank_states, field_list = with_adapters(inputs, frozen_proj, down_proj, up_projection)
    queries, key_rows, value_rows = field_list
    packed = jnp.concatenate([key_rows, value_rows], axis=1).reshape(KEY_VALUE_BLOCKS, BLK, 2 * HQ)
    query_blocks = queries.reshape(KEY_VALUE_BLOCKS, BLK, HQ)
    grad_blocks = grad_out.reshape(KEY_VALUE_BLOCKS, BLK, HQ)

    def per_block(totals, current_block):
        slots = chosen[current_block]
        picked = jnp.take(packed, slots, axis=0)
        usable = (slots != current_block) | (jnp.arange(TOPK, dtype=jnp.int32) == 0)
        attended, dquery, dpacked = block_pass(
            query_blocks[current_block],
            picked[:, :, :HQ].reshape(TOPK * BLK, HQ),
            picked[:, :, HQ:].reshape(TOPK * BLK, HQ),
            grad_blocks[current_block], usable)
        dpacked = dpacked.reshape(TOPK, BLK, 2 * HQ)
        remote = lax.optimization_barrier(dpacked[1:].astype(jnp.bfloat16)).astype(jnp.float32)
        totals = totals.at[current_block].add(dpacked[0])
        totals = totals.at[slots[1:]].add(remote)
        return totals, (attended, dquery.astype(jnp.bfloat16))

    totals, (attended, dquery) = lax.scan(per_block, jnp.zeros((KEY_VALUE_BLOCKS, BLK, 2 * HQ), jnp.float32),
                                          jnp.arange(KEY_VALUE_BLOCKS, dtype=jnp.int32))
    totals = totals.reshape(TOKENS, 2 * HQ)
    grad_fields = jnp.concatenate([dquery.reshape(TOKENS, HQ), totals[:, :HQ].astype(jnp.bfloat16),
                                   totals[:, HQ:].astype(jnp.bfloat16)], axis=1)
    down_terms = []
    up_projection_terms = []
    for group_member in range(3):
        gradient_piece = grad_fields[:, group_member * HQ:(group_member + 1) * HQ]
        up_projection_terms.append(adapter_scale * jnp.dot(low_rank_states[group_member].T, gradient_piece, preferred_element_type=jnp.float32))
        low_rank_gradient = (adapter_scale * jnp.dot(gradient_piece, up_projection[group_member].T, preferred_element_type=jnp.float32)).astype(jnp.bfloat16)
        down_terms.append(jnp.dot(inputs.T, low_rank_gradient, preferred_element_type=jnp.float32))
    return attended.reshape(TOKENS, HQ), grad_fields, jnp.stack(down_terms), jnp.stack(up_projection_terms)


def reference(tokens, projected, down_proj, up_projection, block_ids, cotangent):
    grad_scale = (N_DP * TOKENS) ** -0.5
    outputs = []
    gradients = []
    down_total = jnp.zeros((3, D, R), jnp.float32)
    up_total = jnp.zeros((3, R, HQ), jnp.float32)
    for replica in range(REPLICAS):
        attended, grad_fields, down_terms, up_projection_terms = one_replica(
            tokens[replica], projected[replica], down_proj, up_projection, block_ids[replica], cotangent[replica])
        outputs.append(attended)
        gradients.append(grad_fields)
        down_total = down_total + down_terms
        up_total = up_total + up_projection_terms
    return jnp.stack(outputs), jnp.stack(gradients), grad_scale * down_total, grad_scale * up_total
```

```python
import functools
import math

import jax
import jax.numpy as jnp
from jax import lax
from jax.experimental import pallas as pl
from jax.experimental.pallas import tpu as pltpu
from jax.sharding import PartitionSpec as P

BLK = 256
HD = 128
HEADS = 16
HQ = HEADS * HD
D = 4096
R = 32
ADAPTER_SCALE = 0.5
SCORE_SCALE = HD ** -0.5
LOG2_SCALE = SCORE_SCALE * math.log2(math.e)
GRAD_SCALE = (4 * 16384) ** -0.5
VMEM_BYTES = 50 * 1024 * 1024
NT = (((1,), (1,)), ((), ()))
TN = (((0,), (0,)), ((), ()))
TILES = 32


def place(y, z, core):
    return (y * 8 + z) * 2 + core


def group_row(half, low):
    return low if half == 0 else 3 - low


HEAD_GROUPS = [
    [place(group_row(half, low), z, core) for low in range(2) for z in range(8)]
    for half in range(2)
    for core in range(2)
]
TILE_GROUPS = [[place(y, z, core) for y in range(4) for z in range(8)] for core in range(2)]
CORE_PAIRS = [(i, i ^ 1) for i in range(64)]
TO_LATER = [(place(y, z, c), place(3 - y, z, c)) for y in range(2) for z in range(8) for c in range(2)]
TO_EARLIER = [(b, a) for a, b in TO_LATER]


def to_heads(x):
    return lax.all_to_all(x, "ctx", 0, 0, axis_index_groups=HEAD_GROUPS, tiled=True)


def field_kernel(tok_ref, proj_ref, down_ref, up_ref, out_ref, low_ref, low_s):
    @pl.when(pl.program_id(0) == 0)
    def _():
        low = jnp.dot(tok_ref[...], down_ref[0], preferred_element_type=jnp.float32)
        low_s[...] = low.astype(jnp.bfloat16)
        low_ref[...] = low.astype(jnp.bfloat16)

    adapter = jnp.dot(low_s[...], up_ref[0], preferred_element_type=jnp.float32)
    field = (proj_ref[...].astype(jnp.float32) + ADAPTER_SCALE * adapter).astype(jnp.bfloat16)
    for h in range(4):
        out_ref[h] = field[:, h * HD : (h + 1) * HD]


def make_field(tokens, projected, down_proj, up_projection, m):
    return pl.pallas_call(
        field_kernel,
        grid=(4,),
        in_specs=[
            pl.BlockSpec((BLK, D), lambda i: (0, 0)),
            pl.BlockSpec((BLK, 512), lambda i: (0, m * 4 + i)),
            pl.BlockSpec((1, D, R), lambda i: (m, 0, 0)),
            pl.BlockSpec((1, R, 512), lambda i: (m, 0, i)),
        ],
        out_specs=[
            pl.BlockSpec((4, BLK, HD), lambda i: (i, 0, 0)),
            pl.BlockSpec((BLK, R), lambda i: (0, 0)),
        ],
        out_shape=[
            jax.ShapeDtypeStruct((HEADS, BLK, HD), jnp.bfloat16),
            jax.ShapeDtypeStruct((BLK, R), jnp.bfloat16),
        ],
        scratch_shapes=[pltpu.VMEM((BLK, R), jnp.bfloat16)],
        compiler_params=pltpu.CompilerParams(vmem_limit_bytes=24 * 1024 * 1024),
        cost_estimate=pl.CostEstimate(
            flops=2 * BLK * D * R + 2 * BLK * R * HQ, bytes_accessed=6 * 2**20, transcendentals=0
        ),
        name="field_%d" % m,
    )(tokens, projected, down_proj, up_projection)


def stored_at(block, half, core):
    y = block >> 4
    block_half = y >> 1
    row = jnp.where(block_half == 0, y, 3 - y)
    source = jnp.where(block_half == half, 0, 2) + jnp.where((block & 1) == core, 0, 1)
    return source * 16 + row * 8 + ((block >> 1) & 7)


def slots_of(ids_ref, me_ref, p):
    me = me_ref[0]
    core = me & 1
    half = me >> 5
    low = p >> 3
    y = jnp.where(half == 0, low, 3 - low)
    own = (y * 8 + (p & 7)) * 2 + core
    found = []
    for t in (1, 2):
        block = ids_ref[own * 3 + t]
        bias = jnp.where(block == own, -jnp.inf, 0.0).astype(jnp.float32)
        found.append((stored_at(block, half, core), bias))
    return found


def load_all(sources, targets, sem):
    copies = []
    for source, target in zip(sources, targets):
        for j, ref in enumerate(source):
            copies.append(
                pltpu.make_async_copy(ref, target.at[pl.ds(j * 16, 16)], sem.at[len(copies)])
            )
    for copy in copies:
        copy.start()
    for copy in copies:
        copy.wait()


def transposed_scores(q, keys, biases):
    key_row = lax.broadcasted_iota(jnp.int32, (BLK, BLK), 0)
    query_col = lax.broadcasted_iota(jnp.int32, (BLK, BLK), 1)
    scores = []
    for t in range(3):
        s = lax.dot_general(keys[t], q, NT, preferred_element_type=jnp.float32) * LOG2_SCALE
        if t == 0:
            s = jnp.where(key_row <= query_col, s, -jnp.inf)
        else:
            s = s + biases[t - 1]
        scores.append(s)
    return scores


def forward_kernel(ids_ref, me_ref, q_ref, k0, k1, k2, k3, v0, v1, v2, v3, attn_ref, stat_ref, ks, vs, sem):
    p = pl.program_id(0)

    @pl.when(p == 0)
    def _():
        load_all(((k0, k1, k2, k3), (v0, v1, v2, v3)), (ks, vs), sem)

    (at1, bias1), (at2, bias2) = slots_of(ids_ref, me_ref, p)
    spots = (p, at1, at2)
    scores = transposed_scores(q_ref[0], [ks[i] for i in spots], (bias1, bias2))
    top = jnp.max(jnp.maximum(jnp.maximum(scores[0], scores[1]), scores[2]), axis=0, keepdims=True)
    shifted = [jnp.exp2(s - top) for s in scores]
    inverse = 1.0 / jnp.sum(shifted[0] + shifted[1] + shifted[2], axis=0, keepdims=True)
    out = None
    for t in range(3):
        weights = (shifted[t] * inverse).astype(jnp.bfloat16)
        part = lax.dot_general(vs[spots[t]], weights, TN, preferred_element_type=jnp.float32)
        out = part if out is None else out + part
    attn_ref[0] = out.T.astype(jnp.bfloat16)
    stat_ref[0] = jnp.concatenate([top, inverse, jnp.zeros((6, BLK), jnp.float32)], axis=0)


def backward_kernel(
    ids_ref, me_ref, q_ref, g_ref, attn_ref, stat_ref, k0, k1, k2, k3, v0, v1, v2, v3,
    dq_ref, own_k, own_v, core_k, core_v, far_k, far_v, farcore_k, farcore_v,
    ks, vs, acc_k, acc_v, staged, sem,
):
    p = pl.program_id(0)

    @pl.when(p == 0)
    def _():
        def clear(i, _):
            acc_k[i] = jnp.zeros((BLK, HD), jnp.float32)
            acc_v[i] = jnp.zeros((BLK, HD), jnp.float32)
            return 0

        lax.fori_loop(0, 64, clear, 0)
        load_all(((k0, k1, k2, k3), (v0, v1, v2, v3)), (ks, vs), sem)

    (at1, bias1), (at2, bias2) = slots_of(ids_ref, me_ref, p)
    spots = (p, at1, at2)
    q = q_ref[0]
    g = g_ref[0]
    keys = [ks[i] for i in spots]
    scores = transposed_scores(q, keys, (bias1, bias2))
    top = stat_ref[0, 0:1, :]
    inverse = stat_ref[0, 1:2, :]
    product = attn_ref[0].astype(jnp.float32) * g.astype(jnp.float32)
    delta = jnp.sum(product.T, axis=0, keepdims=True)
    dq = None
    for t in range(3):
        probs = jnp.exp2(scores[t] - top) * inverse
        weights = probs.astype(jnp.bfloat16)
        dprobs = lax.dot_general(vs[spots[t]], g, NT, preferred_element_type=jnp.float32)
        dscores = (probs * (dprobs - delta) * SCORE_SCALE).astype(jnp.bfloat16)
        part = lax.dot_general(keys[t], dscores, TN, preferred_element_type=jnp.float32)
        dq = part if dq is None else dq + part
        dk = jnp.dot(dscores, q, preferred_element_type=jnp.float32)
        dv = jnp.dot(weights, g, preferred_element_type=jnp.float32)
        if t > 0:
            dk = dk.astype(jnp.bfloat16).astype(jnp.float32)
            dv = dv.astype(jnp.bfloat16).astype(jnp.float32)
        acc_k[spots[t]] += dk
        acc_v[spots[t]] += dv
    dq_ref[0] = dq.T.astype(jnp.bfloat16)

    @pl.when(p == 15)
    def _():
        copies = []

        def send(source, target):
            copy = pltpu.make_async_copy(source, target, sem.at[len(copies)])
            copy.start()
            copies.append(copy)

        send(acc_k.at[pl.ds(0, 16)], own_k)
        send(acc_v.at[pl.ds(0, 16)], own_v)
        send(acc_k.at[pl.ds(32, 16)], far_k)
        send(acc_v.at[pl.ds(32, 16)], far_v)

        for n, (acc, at) in enumerate(((acc_k, 48), (acc_v, 48), (acc_k, 16), (acc_v, 16))):
            def cast(i, _, n=n, acc=acc, at=at):
                staged[n * 16 + i] = acc[at + i].astype(jnp.bfloat16)
                return 0

            lax.fori_loop(0, 16, cast, 0)
            send(staged.at[pl.ds(n * 16, 16)], (farcore_k, farcore_v, core_k, core_v)[n])
        for copy in copies:
            copy.wait()


ANY = pl.BlockSpec(memory_space=pl.ANY)


def one_block(rows=BLK, width=HD):
    return pl.BlockSpec((1, rows, width), lambda p, *_: (p, 0, 0))


def blocks_of(kind):
    return jax.ShapeDtypeStruct((16, BLK, HD), kind)


def attend_forward(ids, me, q, keys, values):
    return pl.pallas_call(
        forward_kernel,
        grid_spec=pltpu.PrefetchScalarGridSpec(
            num_scalar_prefetch=2,
            grid=(16,),
            in_specs=[one_block()] + [ANY] * 8,
            out_specs=[one_block(), one_block(8, BLK)],
            scratch_shapes=[
                pltpu.VMEM((64, BLK, HD), jnp.bfloat16),
                pltpu.VMEM((64, BLK, HD), jnp.bfloat16),
                pltpu.SemaphoreType.DMA((8,)),
            ],
        ),
        out_shape=[blocks_of(jnp.bfloat16), jax.ShapeDtypeStruct((16, 8, BLK), jnp.float32)],
        compiler_params=pltpu.CompilerParams(vmem_limit_bytes=VMEM_BYTES),
        cost_estimate=pl.CostEstimate(
            flops=16 * 2 * 2 * BLK * 3 * BLK * HD, bytes_accessed=11 * 2**20, transcendentals=16 * 3 * BLK * BLK
        ),
        name="attend_forward",
    )(ids, me, q, *keys, *values)


def attend_backward(ids, me, q, g, attn, stats, keys, values):
    wide = blocks_of(jnp.float32)
    narrow = blocks_of(jnp.bfloat16)
    return pl.pallas_call(
        backward_kernel,
        grid_spec=pltpu.PrefetchScalarGridSpec(
            num_scalar_prefetch=2,
            grid=(16,),
            in_specs=[one_block(), one_block(), one_block(), one_block(8, BLK)] + [ANY] * 8,
            out_specs=[one_block()] + [ANY] * 8,
            scratch_shapes=[
                pltpu.VMEM((64, BLK, HD), jnp.bfloat16),
                pltpu.VMEM((64, BLK, HD), jnp.bfloat16),
                pltpu.VMEM((64, BLK, HD), jnp.float32),
                pltpu.VMEM((64, BLK, HD), jnp.float32),
                pltpu.VMEM((64, BLK, HD), jnp.bfloat16),
                pltpu.SemaphoreType.DMA((8,)),
            ],
        ),
        out_shape=[narrow, wide, wide, narrow, narrow, wide, wide, narrow, narrow],
        compiler_params=pltpu.CompilerParams(vmem_limit_bytes=VMEM_BYTES),
        cost_estimate=pl.CostEstimate(
            flops=16 * 5 * 2 * BLK * 3 * BLK * HD, bytes_accessed=24 * 2**20, transcendentals=16 * 3 * BLK * BLK
        ),
        name="attend_backward",
    )(ids, me, q, g, attn, stats, *keys, *values)


def grads_kernel(first, me_ref, *refs):
    if first:
        g_ref, tok_ref, low_ref, up_ref, gp_ref, keep_ref, send_ref, terms = refs
    else:
        _, g_ref, tok_ref, low_ref, up_ref, gp_ref, keep_ref, send_ref, terms = refs
    dlow = None
    low = low_ref[...]
    for h in range(HEADS):
        g = g_ref[h]
        cols = slice(h * HD, (h + 1) * HD)
        gp_ref[:, cols] = g
        part = lax.dot_general(up_ref[0, :, cols], g, NT, preferred_element_type=jnp.float32)
        dlow = part if dlow is None else dlow + part
        up_term = jnp.dot(low, g, preferred_element_type=jnp.float32) * (ADAPTER_SCALE * GRAD_SCALE)
        for side in range(2):
            cut = up_term[:, side * 64 : (side + 1) * 64]
            terms[2 * h + side, 32:48, :] = jnp.concatenate([cut[0:16], cut[16:32]], axis=1)
    dlow = (dlow * ADAPTER_SCALE).astype(jnp.bfloat16)
    for t in range(TILES):
        down_term = jnp.dot(dlow, tok_ref[:, t * 128 : (t + 1) * 128], preferred_element_type=jnp.float32)
        terms[t, 0:32, :] = down_term * GRAD_SCALE
    core = me_ref[0] & 1

    @pl.when(core == 0)
    def _():
        keep_ref[...] = terms[:, 0:24, :]
        send_ref[...] = terms[:, 24:48, :]

    @pl.when(core == 1)
    def _():
        keep_ref[...] = terms[:, 24:48, :]
        send_ref[...] = terms[:, 0:24, :]


def member_grads(me, grad_proj, g, tokens, low, up_projection, m):
    first = grad_proj is None
    piece = jax.ShapeDtypeStruct((TILES, 24, 128), jnp.float32)
    whole = lambda *shape: pl.BlockSpec(shape, lambda i, *_: (0,) * len(shape))
    in_specs = [
        whole(HEADS, BLK, HD),
        whole(BLK, D),
        whole(R, BLK),
        pl.BlockSpec((1, R, HQ), lambda i, *_: (m, 0, 0)),
    ]
    operands = [g, tokens, low, up_projection]
    if not first:
        in_specs = [ANY] + in_specs
        operands = [grad_proj] + operands
    return pl.pallas_call(
        functools.partial(grads_kernel, first),
        grid_spec=pltpu.PrefetchScalarGridSpec(
            num_scalar_prefetch=1,
            grid=(1,),
            in_specs=in_specs,
            out_specs=[
                pl.BlockSpec((BLK, HQ), lambda i, *_: (0, m)),
                whole(TILES, 24, 128),
                whole(TILES, 24, 128),
            ],
            scratch_shapes=[pltpu.VMEM((TILES, 48, 128), jnp.float32)],
        ),
        out_shape=[jax.ShapeDtypeStruct((BLK, 3 * HQ), jnp.bfloat16), piece, piece],
        input_output_aliases={} if first else {1: 0},
        compiler_params=pltpu.CompilerParams(vmem_limit_bytes=24 * 1024 * 1024),
        cost_estimate=pl.CostEstimate(
            flops=2 * BLK * R * (D + 2 * HQ), bytes_accessed=5 * 2**20, transcendentals=0
        ),
        name="grads_%d" % m,
    )(me, *operands)


def shards(tokens, projected, down_proj, up_projection, block_ids, cotangent):
    tokens = tokens[0]
    projected = projected[0]
    me = lax.axis_index("ctx").astype(jnp.int32)
    core = me & 1
    lane = core * 4 + lax.axis_index("dp")
    me = me.reshape(1)
    ids = block_ids[0].reshape(-1)

    swap = lambda x: lax.ppermute(x, "ctx", CORE_PAIRS)
    later = lambda x: lax.ppermute(x, "ctx", TO_LATER)
    earlier = lambda x: lax.ppermute(x, "ctx", TO_EARLIER)

    field_k, low_k = make_field(tokens, projected, down_proj, up_projection, 1)
    field_v, low_v = make_field(tokens, projected, down_proj, up_projection, 2)
    field_q, low_q = make_field(tokens, projected, down_proj, up_projection, 0)
    grad_heads = jnp.transpose(cotangent[0].reshape(BLK, HEADS, HD), (1, 0, 2))

    key = to_heads(field_k)
    field_v, key = lax.optimization_barrier((field_v, key))
    key_far = later(key)
    key_core = swap(key)
    value = to_heads(field_v)
    field_q, value = lax.optimization_barrier((field_q, value))
    value_far = later(value)
    value_core = swap(value)
    query = to_heads(field_q)
    grad_heads, query = lax.optimization_barrier((grad_heads, query))
    keys = (key, key_core, key_far, swap(key_far))
    values = (value, value_core, value_far, swap(value_far))
    grad = to_heads(grad_heads)

    attn, stats = attend_forward(ids, me, query, keys, values)
    dq, own_k, own_v, core_k, core_v, far_k, far_v, farcore_k, farcore_v = attend_backward(
        ids, me, query, grad, attn, stats, keys, values
    )
    attn_home = to_heads(attn)
    dq, attn_home = lax.optimization_barrier((dq, attn_home))
    dq_home = to_heads(dq)

    def gather_parts(own, core_part, far, farcore):
        far_sum = (far + swap(farcore).astype(jnp.float32)).astype(jnp.bfloat16)
        returned = earlier(far_sum)
        total = own + swap(core_part).astype(jnp.float32) + returned.astype(jnp.float32)
        return total.astype(jnp.bfloat16)

    dk = gather_parts(own_k, core_k, far_k, farcore_k)
    dv = gather_parts(own_v, core_v, far_v, farcore_v)
    dk, dq_home = lax.optimization_barrier((dk, dq_home))
    dk_home = to_heads(dk)
    dv, dk_home = lax.optimization_barrier((dv, dk_home))
    dv_home = to_heads(dv)

    attn_rows = jnp.transpose(attn_home, (1, 0, 2)).reshape(BLK, HQ)
    grad_proj, keep_q, send_q = member_grads(me, None, dq_home, tokens, low_q.T, up_projection, 0)
    grad_proj, keep_k, send_k = member_grads(me, grad_proj, dk_home, tokens, low_k.T, up_projection, 1)
    grad_proj, keep_v, send_v = member_grads(me, grad_proj, dv_home, tokens, low_v.T, up_projection, 2)

    pieces = jnp.concatenate(
        [keep_q + swap(send_q), keep_k + swap(send_k), keep_v + swap(send_v)], axis=1
    )
    pieces = lax.all_to_all(pieces, "ctx", 0, 0, axis_index_groups=TILE_GROUPS, tiled=True)
    mine = jnp.sum(pieces, axis=0)
    others = [
        lax.ppermute(mine, "dp", [(j, (j + step) % 4) for j in range(4)]) for step in (1, 2, 3)
    ]
    mine = (mine + others[0]) + (others[1] + others[2])
    other = swap(mine)
    low_rows = jnp.where(core == 0, mine, other).reshape(3, 24, 128)
    high_rows = jnp.where(core == 0, other, mine).reshape(3, 24, 128)
    full = jnp.concatenate([low_rows, high_rows], axis=1)
    down_piece = lax.dynamic_slice_in_dim(full[:, 0:32], lane * 16, 16, axis=2)
    up_low = lax.dynamic_slice_in_dim(full[:, 32:48, 0:64], lane * 8, 8, axis=2)
    up_high = lax.dynamic_slice_in_dim(full[:, 32:48, 64:128], lane * 8, 8, axis=2)
    grad_down = jnp.transpose(down_piece, (0, 2, 1))
    grad_up = jnp.concatenate([up_low, up_high], axis=1)
    return attn_rows[None], grad_proj[None], grad_down, grad_up


def solution(mesh):
    placed = (
        P("dp", "ctx", None),
        P("dp", "ctx", None),
        P(),
        P(),
        P("dp", None, None),
        P("dp", "ctx", None),
    )
    return jax.shard_map(
        shards,
        mesh=mesh,
        in_specs=placed,
        out_specs=(
            P("dp", "ctx", None),
            P("dp", "ctx", None),
            P(None, ("ctx", "dp"), None),
            P(None, None, ("ctx", "dp")),
        ),
        check_vma=False,
    )
```

```python
import math

import jax
import jax.numpy as jnp
from jax import lax
from jax.experimental import pallas as pl
from jax.experimental.pallas import tpu as pltpu
from jax.sharding import PartitionSpec as P

BLK = 256
HD = 128
HEADS = 16
HQ = HEADS * HD
D = 4096
R = 32
ADAPTER_SCALE = 0.5
SCORE_SCALE = HD ** -0.5
LOG2_SCALE = SCORE_SCALE * math.log2(math.e)
GRAD_SCALE = (4 * 16384) ** -0.5
VMEM_BYTES = 56 * 1024 * 1024
NT = (((1,), (1,)), ((), ()))
TN = (((0,), (0,)), ((), ()))
TILES = 32
PER_STEP = 4


def place(y, z, core):
    return (y * 8 + z) * 2 + core


def group_row(half, low):
    return low if half == 0 else 3 - low


EVERY = [(y, z, c) for y in range(4) for z in range(8) for c in range(2)]
HEAD_GROUPS = [
    [place(group_row(half, low), z, core) for low in range(2) for z in range(8)]
    for half in range(2)
    for core in range(2)
]
CORE_PAIRS = [(i, i ^ 1) for i in range(64)]
TO_LATER = [(place(y, z, c), place(3 - y, z, c)) for y, z, c in EVERY if y < 2]
TO_EARLIER = [(b, a) for a, b in TO_LATER]
TILE_GROUPS = [[place(y, z, core) for y in range(4) for z in range(8)] for core in range(2)]


def to_heads(x):
    return lax.all_to_all(x, "ctx", 0, 0, axis_index_groups=HEAD_GROUPS, tiled=True)


def swap(x):
    return lax.ppermute(x, "ctx", CORE_PAIRS)


def after(x, first):
    return lax.optimization_barrier((x, first))


def whole(*shape):
    return pl.BlockSpec(shape, lambda i, *_: (0,) * len(shape))


def add_adapter(proj, low, up):
    adapter = jnp.dot(low, up, preferred_element_type=jnp.float32)
    return (proj.astype(jnp.float32) + ADAPTER_SCALE * adapter).astype(jnp.bfloat16)


def key_value_kernel(tok_ref, down_ref, k_ref, v_ref, up_ref, out_ref, low_ref, low_s):
    @pl.when(pl.program_id(0) == 0)
    def _():
        low = lax.dot_general(
            tok_ref[...], down_ref[...].reshape(3 * R, D), NT, preferred_element_type=jnp.float32
        )
        low_s[...] = low.astype(jnp.bfloat16)
        low_ref[...] = low.astype(jnp.bfloat16)

    low = low_s[...]
    for side, ref in enumerate((k_ref, v_ref)):
        m = side + 1
        field = add_adapter(ref[...], low[:, m * R : (m + 1) * R], up_ref[m])
        for h in range(8):
            out_ref[h, side] = field[:, h * HD : (h + 1) * HD]


def make_key_value(tokens, projected, down_t, up_projection):
    return pl.pallas_call(
        key_value_kernel,
        grid=(2,),
        in_specs=[
            whole(BLK, D),
            whole(3, R, D),
            pl.BlockSpec((BLK, 1024), lambda i: (0, 2 + i)),
            pl.BlockSpec((BLK, 1024), lambda i: (0, 4 + i)),
            pl.BlockSpec((3, R, 1024), lambda i: (0, 0, i)),
        ],
        out_specs=[pl.BlockSpec((8, 2, BLK, HD), lambda i: (i, 0, 0, 0)), whole(BLK, 3 * R)],
        out_shape=[
            jax.ShapeDtypeStruct((HEADS, 2, BLK, HD), jnp.bfloat16),
            jax.ShapeDtypeStruct((BLK, 3 * R), jnp.bfloat16),
        ],
        scratch_shapes=[pltpu.VMEM((BLK, 3 * R), jnp.bfloat16)],
        compiler_params=pltpu.CompilerParams(vmem_limit_bytes=VMEM_BYTES),
        cost_estimate=pl.CostEstimate(
            flops=2 * BLK * D * 3 * R + 4 * BLK * R * HQ, bytes_accessed=7 * 2**20, transcendentals=0
        ),
        name="make_key_value",
    )(tokens, down_t, projected, projected, up_projection)


def query_kernel(low_ref, proj_ref, up_ref, cot_ref, out_ref):
    field = add_adapter(proj_ref[...], low_ref[:, 0:R], up_ref[0])
    for h in range(4):
        cols = slice(h * HD, (h + 1) * HD)
        out_ref[h, 0] = field[:, cols]
        out_ref[h, 1] = cot_ref[:, cols]


def make_query(low, projected, up_projection, cotangent):
    return pl.pallas_call(
        query_kernel,
        grid=(4,),
        in_specs=[
            whole(BLK, 3 * R),
            pl.BlockSpec((BLK, 512), lambda i: (0, i)),
            pl.BlockSpec((1, R, 512), lambda i: (0, 0, i)),
            pl.BlockSpec((BLK, 512), lambda i: (0, i)),
        ],
        out_specs=pl.BlockSpec((4, 2, BLK, HD), lambda i: (i, 0, 0, 0)),
        out_shape=jax.ShapeDtypeStruct((HEADS, 2, BLK, HD), jnp.bfloat16),
        compiler_params=pltpu.CompilerParams(vmem_limit_bytes=VMEM_BYTES),
        cost_estimate=pl.CostEstimate(
            flops=2 * BLK * R * HQ, bytes_accessed=4 * 2**20, transcendentals=0
        ),
        name="make_query",
    )(low, projected, up_projection, cotangent)


def stored_at(block, half, core):
    y = block >> 4
    block_half = y >> 1
    row = jnp.where(block_half == 0, y, 3 - y)
    source = jnp.where(block_half == half, 0, 2) + jnp.where((block & 1) == core, 0, 1)
    return source * 16 + row * 8 + ((block >> 1) & 7)


def slots_of(ids_ref, me_ref, p):
    me = me_ref[0]
    core = me & 1
    half = me >> 5
    low = p >> 3
    y = jnp.where(half == 0, low, 3 - low)
    own = (y * 8 + (p & 7)) * 2 + core
    spots = [p]
    biases = [None]
    for t in (1, 2):
        block = ids_ref[own * 3 + t]
        spots.append(stored_at(block, half, core))
        biases.append(jnp.where(block == own, -jnp.inf, 0.0).astype(jnp.float32))
    return spots, biases


def attend_kernel(
    ids_ref, me_ref, qg_ref, kv0, kv1, kv2, kv3,
    out_ref, own_ref, far_ref, core_ref, farcore_ref, kvs, acc, staged, sem,
):
    step = pl.program_id(0)

    @pl.when(step == 0)
    def _():
        copies = [
            pltpu.make_async_copy(ref, kvs.at[pl.ds(16 * n, 16)], sem.at[n])
            for n, ref in enumerate((kv0, kv1, kv2, kv3))
        ]
        for copy in copies:
            copy.start()

        def clear(i, _):
            acc[i] = jnp.zeros((2, BLK, HD), jnp.float32)
            return 0

        lax.fori_loop(0, 64, clear, 0)
        for copy in copies:
            copy.wait()

    key_row = lax.broadcasted_iota(jnp.int32, (BLK, BLK), 0)
    query_col = lax.broadcasted_iota(jnp.int32, (BLK, BLK), 1)
    causal = key_row <= query_col
    work = []
    for sub in range(PER_STEP):
        spots, biases = slots_of(ids_ref, me_ref, step * PER_STEP + sub)
        work.append((spots, biases, qg_ref[sub, 0], qg_ref[sub, 1]))
    scores = []
    for spots, biases, q, g in work:
        parts = []
        for t in range(3):
            s = lax.dot_general(kvs[spots[t], 0], q, NT, preferred_element_type=jnp.float32)
            s = s * LOG2_SCALE
            parts.append(jnp.where(causal, s, -jnp.inf) if t == 0 else s + biases[t])
        scores.append(parts)
    middle = []
    for (spots, biases, q, g), s in zip(work, scores):
        top = jnp.max(jnp.maximum(jnp.maximum(s[0], s[1]), s[2]), axis=0, keepdims=True)
        shifted = [jnp.exp2(x - top) for x in s]
        inverse = 1.0 / jnp.sum(shifted[0] + shifted[1] + shifted[2], axis=0, keepdims=True)
        probs = [x * inverse for x in shifted]
        weights = [x.astype(jnp.bfloat16) for x in probs]
        out = None
        for t in range(3):
            part = lax.dot_general(kvs[spots[t], 1], weights[t], TN, preferred_element_type=jnp.float32)
            out = part if out is None else out + part
        middle.append((probs, weights, out))
    for sub in range(PER_STEP):
        spots, biases, q, g = work[sub]
        probs, weights, out = middle[sub]
        attn = out.T.astype(jnp.bfloat16)
        out_ref[sub, 0] = attn
        product = attn.astype(jnp.float32) * g.astype(jnp.float32)
        delta = jnp.sum(product.T, axis=0, keepdims=True)
        dq = None
        for t in range(3):
            dprobs = lax.dot_general(kvs[spots[t], 1], g, NT, preferred_element_type=jnp.float32)
            dscores = (probs[t] * (dprobs - delta) * SCORE_SCALE).astype(jnp.bfloat16)
            part = lax.dot_general(kvs[spots[t], 0], dscores, TN, preferred_element_type=jnp.float32)
            dq = part if dq is None else dq + part
            dk = jnp.dot(dscores, q, preferred_element_type=jnp.float32)
            dv = jnp.dot(weights[t], g, preferred_element_type=jnp.float32)
            if t > 0:
                dk = dk.astype(jnp.bfloat16).astype(jnp.float32)
                dv = dv.astype(jnp.bfloat16).astype(jnp.float32)
            acc[spots[t], 0] += dk
            acc[spots[t], 1] += dv
        out_ref[sub, 1] = dq.T.astype(jnp.bfloat16)

    @pl.when(step == pl.num_programs(0) - 1)
    def _():
        copies = []

        def send(source, target):
            copy = pltpu.make_async_copy(source, target, sem.at[len(copies)])
            copy.start()
            copies.append(copy)

        for n, (at, target) in enumerate(((48, farcore_ref), (16, core_ref))):

            def cast(i, _, n=n, at=at):
                staged[n * 16 + i] = acc[at + i].astype(jnp.bfloat16)
                return 0

            if n == 1:
                send(acc.at[pl.ds(32, 16)], far_ref)
                send(acc.at[pl.ds(0, 16)], own_ref)
            lax.fori_loop(0, 16, cast, 0)
            send(staged.at[pl.ds(n * 16, 16)], target)
        for copy in copies:
            copy.wait()


ANY = pl.BlockSpec(memory_space=pl.ANY)


def attend(ids, me, query, key_values):
    wide = jax.ShapeDtypeStruct((16, 2, BLK, HD), jnp.float32)
    narrow = jax.ShapeDtypeStruct((16, 2, BLK, HD), jnp.bfloat16)
    rows = pl.BlockSpec((PER_STEP, 2, BLK, HD), lambda p, *_: (p, 0, 0, 0))
    return pl.pallas_call(
        attend_kernel,
        grid_spec=pltpu.PrefetchScalarGridSpec(
            num_scalar_prefetch=2,
            grid=(16 // PER_STEP,),
            in_specs=[rows] + [ANY] * 4,
            out_specs=[rows] + [ANY] * 4,
            scratch_shapes=[
                pltpu.VMEM((64, 2, BLK, HD), jnp.bfloat16),
                pltpu.VMEM((64, 2, BLK, HD), jnp.float32),
                pltpu.VMEM((32, 2, BLK, HD), jnp.bfloat16),
                pltpu.SemaphoreType.DMA((4,)),
            ],
        ),
        out_shape=[narrow, wide, wide, narrow, narrow],
        compiler_params=pltpu.CompilerParams(vmem_limit_bytes=VMEM_BYTES),
        cost_estimate=pl.CostEstimate(
            flops=16 * 6 * 2 * BLK * 3 * BLK * HD,
            bytes_accessed=26 * 2**20,
            transcendentals=16 * 3 * BLK * BLK,
        ),
        name="attend",
    )(ids, me, query, *key_values)


def write_terms(terms, base, head, tok_ref, low, up):
    dlow = None
    for h in range(HEADS):
        g = head(h)
        cols = slice(h * HD, (h + 1) * HD)
        part = lax.dot_general(up[:, cols], g, NT, preferred_element_type=jnp.float32)
        dlow = part if dlow is None else dlow + part
        up_term = jnp.dot(low, g, preferred_element_type=jnp.float32) * (ADAPTER_SCALE * GRAD_SCALE)
        for side in range(2):
            cut = up_term[:, side * 64 : (side + 1) * 64]
            terms[2 * h + side, base + 32 : base + 48, :] = jnp.concatenate([cut[0:16], cut[16:32]], axis=1)
    dlow = (dlow * ADAPTER_SCALE).astype(jnp.bfloat16)
    for t in range(TILES):
        down_term = jnp.dot(dlow, tok_ref[:, t * 128 : (t + 1) * 128], preferred_element_type=jnp.float32)
        terms[t, base : base + 32, :] = down_term * GRAD_SCALE


def query_grads_kernel(home_ref, tok_ref, low_ref, up_ref, attn_ref, gp_ref, terms):
    for h in range(HEADS):
        cols = slice(h * HD, (h + 1) * HD)
        attn_ref[:, cols] = home_ref[h, 0]
        gp_ref[:, cols] = home_ref[h, 1]
    write_terms(terms, 0, lambda h: home_ref[h, 1], tok_ref, low_ref[...], up_ref[0])


def key_value_grads_kernel(
    me_ref, _, other_ref, home_ref, tok_ref, low_ref, up_ref, gp_ref, keep_ref, send_ref, terms, rows, sem
):
    for side in range(2):
        for h in range(HEADS):
            rows[:, side * HQ + h * HD : side * HQ + (h + 1) * HD] = home_ref[h, side]
    copy = pltpu.make_async_copy(rows, gp_ref.at[:, pl.ds(HQ, 2 * HQ)], sem)
    copy.start()
    for side in range(2):
        write_terms(
            terms,
            side * 48,
            lambda h: home_ref[h, side],
            tok_ref,
            low_ref[(side + 1) * R : (side + 2) * R, :],
            up_ref[side + 1],
        )

    def first(ref):
        ref[:, 0:48, :] = other_ref[...]
        ref[:, 48:72, :] = terms[:, 0:24, :]

    def second(ref):
        ref[...] = terms[:, 24:96, :]

    core = me_ref[0] & 1

    @pl.when(core == 0)
    def _():
        first(keep_ref)
        second(send_ref)

    @pl.when(core == 1)
    def _():
        first(send_ref)
        second(keep_ref)

    copy.wait()


def query_grads(home, tokens, low_t, up_projection):
    return pl.pallas_call(
        query_grads_kernel,
        grid=(1,),
        in_specs=[
            whole(HEADS, 2, BLK, HD),
            whole(BLK, D),
            whole(R, BLK),
            whole(1, R, HQ),
        ],
        out_specs=[whole(BLK, HQ), whole(BLK, HQ), whole(TILES, 48, 128)],
        out_shape=[
            jax.ShapeDtypeStruct((BLK, HQ), jnp.bfloat16),
            jax.ShapeDtypeStruct((BLK, 3 * HQ), jnp.bfloat16),
            jax.ShapeDtypeStruct((TILES, 48, 128), jnp.float32),
        ],
        compiler_params=pltpu.CompilerParams(vmem_limit_bytes=24 * 1024 * 1024),
        cost_estimate=pl.CostEstimate(
            flops=2 * BLK * R * (D + 2 * HQ), bytes_accessed=8 * 2**20, transcendentals=0
        ),
        name="query_grads",
    )(home, tokens, low_t, up_projection)


def key_value_grads(me, grad_proj, terms_q, home, tokens, low_t, up_projection):
    piece = jax.ShapeDtypeStruct((TILES, 72, 128), jnp.float32)
    return pl.pallas_call(
        key_value_grads_kernel,
        grid_spec=pltpu.PrefetchScalarGridSpec(
            num_scalar_prefetch=1,
            grid=(1,),
            in_specs=[
                ANY,
                whole(TILES, 48, 128),
                whole(HEADS, 2, BLK, HD),
                whole(BLK, D),
                whole(3 * R, BLK),
                whole(3, R, HQ),
            ],
            out_specs=[
                ANY,
                whole(TILES, 72, 128),
                whole(TILES, 72, 128),
            ],
            scratch_shapes=[
                pltpu.VMEM((TILES, 96, 128), jnp.float32),
                pltpu.VMEM((BLK, 2 * HQ), jnp.bfloat16),
                pltpu.SemaphoreType.DMA,
            ],
        ),
        out_shape=[jax.ShapeDtypeStruct((BLK, 3 * HQ), jnp.bfloat16), piece, piece],
        input_output_aliases={1: 0},
        compiler_params=pltpu.CompilerParams(vmem_limit_bytes=28 * 1024 * 1024),
        cost_estimate=pl.CostEstimate(
            flops=4 * BLK * R * (D + 2 * HQ), bytes_accessed=10 * 2**20, transcendentals=0
        ),
        name="key_value_grads",
    )(me, grad_proj, terms_q, home, tokens, low_t, up_projection)


def finish_kernel(lane_ref, mine_ref, other_ref, down_ref, up_ref, full, down_t, up_t):
    lane = lane_ref[0]

    @pl.when(lane < 4)
    def _():
        full[0:72] = mine_ref[...]
        full[72:144] = other_ref[...]

    @pl.when(lane >= 4)
    def _():
        full[0:72] = other_ref[...]
        full[72:144] = mine_ref[...]

    for m in range(3):
        down_t[...] = full[m * 48 : m * 48 + 32, :].T
        down_ref[m] = down_t[pl.ds(lane * 16, 16), :]
        up_t[...] = full[m * 48 + 32 : m * 48 + 48, :].T
        up_ref[m, :, 0:16] = up_t[pl.ds(lane * 8, 8), :]
        up_ref[m, :, 16:32] = up_t[pl.ds(lane * 8 + 64, 8), :]


def finish(lane, mine, other):
    return pl.pallas_call(
        finish_kernel,
        grid_spec=pltpu.PrefetchScalarGridSpec(
            num_scalar_prefetch=1,
            grid=(1,),
            in_specs=[whole(72, 128), whole(72, 128)],
            out_specs=[whole(3, 16, R), whole(3, 8, R)],
            scratch_shapes=[
                pltpu.VMEM((144, 128), jnp.float32),
                pltpu.VMEM((128, R), jnp.float32),
                pltpu.VMEM((128, 16), jnp.float32),
            ],
        ),
        out_shape=[
            jax.ShapeDtypeStruct((3, 16, R), jnp.float32),
            jax.ShapeDtypeStruct((3, 8, R), jnp.float32),
        ],
        compiler_params=pltpu.CompilerParams(vmem_limit_bytes=8 * 1024 * 1024),
        name="finish",
    )(lane, mine, other)


def shards(tokens, projected, down_proj, up_projection, block_ids, cotangent):
    tokens = tokens[0]
    projected = projected[0]
    me = lax.axis_index("ctx").astype(jnp.int32)
    lane = ((me & 1) * 4 + lax.axis_index("dp")).astype(jnp.int32).reshape(1)
    me = me.reshape(1)
    ids = block_ids[0].reshape(-1)

    local, low = make_key_value(tokens, projected, jnp.transpose(down_proj, (0, 2, 1)), up_projection)
    key_value = to_heads(local)
    local = make_query(low, projected, up_projection, cotangent[0])
    low_t = low.T
    local, key_value = after(local, key_value)
    far = lax.ppermute(key_value, "ctx", TO_LATER)
    query = to_heads(local)
    out, own, far_part, core_part, farcore_part = attend(
        ids, me, query, (key_value, swap(key_value), far, swap(far))
    )

    far_sum = (far_part + swap(farcore_part).astype(jnp.float32)).astype(jnp.bfloat16)
    returned = lax.ppermute(far_sum, "ctx", TO_EARLIER)
    out_home = to_heads(out)
    total = own + swap(core_part).astype(jnp.float32) + returned.astype(jnp.float32)
    total, out_home = after(total.astype(jnp.bfloat16), out_home)
    total_home = to_heads(total)
    attn_rows, grad_proj, terms_q = query_grads(out_home, tokens, low_t, up_projection)
    grad_proj, keep, send = key_value_grads(
        me, grad_proj, terms_q, total_home, tokens, low_t, up_projection
    )
    pieces = (keep + swap(send)).astype(jnp.bfloat16)
    pieces = lax.all_to_all(pieces, "ctx", 0, 0, axis_index_groups=TILE_GROUPS, tiled=True)
    mine = jnp.sum(pieces.astype(jnp.float32), axis=0)
    others = [
        lax.ppermute(mine, "dp", [(j, (j + step) % 4) for j in range(4)]) for step in (1, 2, 3)
    ]
    mine = (mine + others[0]) + (others[1] + others[2])
    grad_down, grad_up = finish(lane, mine, swap(mine))
    return attn_rows[None], grad_proj[None], grad_down, jnp.transpose(grad_up, (0, 2, 1))


def solution(mesh):
    placed = (
        P("dp", "ctx", None),
        P("dp", "ctx", None),
        P(),
        P(),
        P("dp", None, None),
        P("dp", "ctx", None),
    )
    return jax.shard_map(
        shards,
        mesh=mesh,
        in_specs=placed,
        out_specs=(
            P("dp", "ctx", None),
            P("dp", "ctx", None),
            P(None, ("ctx", "dp"), None),
            P(None, None, ("ctx", "dp")),
        ),
        check_vma=False,
    )
```

```python
import math

import jax
import jax.numpy as jnp
from jax import lax
from jax.experimental import pallas as pl
from jax.experimental.pallas import tpu as pltpu
from jax.sharding import PartitionSpec as P

BLK = 256
HD = 128
HEADS = 16
HQ = HEADS * HD
D = 4096
R = 32
ADAPTER_SCALE = 0.5
SCORE_SCALE = HD ** -0.5
LOG2_SCALE = SCORE_SCALE * math.log2(math.e)
GRAD_SCALE = (4 * 16384) ** -0.5
VMEM_BYTES = 56 * 1024 * 1024
NT = (((1,), (1,)), ((), ()))
TN = (((0,), (0,)), ((), ()))
TILES = 32
PER_STEP = 4
STEPS = 4


def place(y, z, core):
    return (y * 8 + z) * 2 + core


def group_row(half, low):
    return low if half == 0 else 3 - low


EVERY = [(y, z, c) for y in range(4) for z in range(8) for c in range(2)]
HEAD_GROUPS = [
    [place(group_row(half, low), z, core) for low in range(2) for z in range(8)]
    for half in range(2)
    for core in range(2)
]
CORE_PAIRS = [(i, i ^ 1) for i in range(64)]
TO_LATER = [(place(y, z, c), place(3 - y, z, c)) for y, z, c in EVERY if y < 2]
TO_EARLIER = [(b, a) for a, b in TO_LATER]
TILE_GROUPS = [[place(y, z, core) for y in range(4) for z in range(8)] for core in range(2)]


def to_heads(x):
    return lax.all_to_all(x, "ctx", 0, 0, axis_index_groups=HEAD_GROUPS, tiled=True)


def swap(x):
    return lax.ppermute(x, "ctx", CORE_PAIRS)


def after(x, first):
    return lax.optimization_barrier((x, first))


def whole(*shape):
    return pl.BlockSpec(shape, lambda i, *_: (0,) * len(shape))


def add_adapter(proj, low, up):
    adapter = jnp.dot(low, up, preferred_element_type=jnp.float32)
    return (proj.astype(jnp.float32) + ADAPTER_SCALE * adapter).astype(jnp.bfloat16)


def key_value_kernel(tok_ref, down_ref, k_ref, v_ref, up_ref, out_ref, low_ref, low_s):
    @pl.when(pl.program_id(0) == 0)
    def _():
        low = lax.dot_general(
            tok_ref[...], down_ref[...].reshape(3 * R, D), NT, preferred_element_type=jnp.float32
        )
        low_s[...] = low.astype(jnp.bfloat16)
        low_ref[...] = low.astype(jnp.bfloat16)

    low = low_s[...]
    for side, ref in enumerate((k_ref, v_ref)):
        m = side + 1
        field = add_adapter(ref[...], low[:, m * R : (m + 1) * R], up_ref[m])
        for h in range(8):
            out_ref[h, side] = field[:, h * HD : (h + 1) * HD]


def make_key_value(tokens, projected, down_t, up_projection):
    return pl.pallas_call(
        key_value_kernel,
        grid=(2,),
        in_specs=[
            whole(BLK, D),
            whole(3, R, D),
            pl.BlockSpec((BLK, 1024), lambda i: (0, 2 + i)),
            pl.BlockSpec((BLK, 1024), lambda i: (0, 4 + i)),
            pl.BlockSpec((3, R, 1024), lambda i: (0, 0, i)),
        ],
        out_specs=[pl.BlockSpec((8, 2, BLK, HD), lambda i: (i, 0, 0, 0)), whole(BLK, 3 * R)],
        out_shape=[
            jax.ShapeDtypeStruct((HEADS, 2, BLK, HD), jnp.bfloat16),
            jax.ShapeDtypeStruct((BLK, 3 * R), jnp.bfloat16),
        ],
        scratch_shapes=[pltpu.VMEM((BLK, 3 * R), jnp.bfloat16)],
        compiler_params=pltpu.CompilerParams(vmem_limit_bytes=VMEM_BYTES),
        cost_estimate=pl.CostEstimate(
            flops=2 * BLK * D * 3 * R + 4 * BLK * R * HQ, bytes_accessed=7 * 2**20, transcendentals=0
        ),
        name="make_key_value",
    )(tokens, down_t, projected, projected, up_projection)


def query_kernel(low_ref, proj_ref, up_ref, cot_ref, out_ref):
    field = add_adapter(proj_ref[...], low_ref[:, 0:R], up_ref[0])
    for h in range(4):
        cols = slice(h * HD, (h + 1) * HD)
        out_ref[h, 0] = field[:, cols]
        out_ref[h, 1] = cot_ref[:, cols]


def make_query(low, projected, up_projection, cotangent):
    return pl.pallas_call(
        query_kernel,
        grid=(4,),
        in_specs=[
            whole(BLK, 3 * R),
            pl.BlockSpec((BLK, 512), lambda i: (0, i)),
            pl.BlockSpec((1, R, 512), lambda i: (0, 0, i)),
            pl.BlockSpec((BLK, 512), lambda i: (0, i)),
        ],
        out_specs=pl.BlockSpec((4, 2, BLK, HD), lambda i: (i, 0, 0, 0)),
        out_shape=jax.ShapeDtypeStruct((HEADS, 2, BLK, HD), jnp.bfloat16),
        compiler_params=pltpu.CompilerParams(vmem_limit_bytes=VMEM_BYTES),
        cost_estimate=pl.CostEstimate(
            flops=2 * BLK * R * HQ, bytes_accessed=4 * 2**20, transcendentals=0
        ),
        name="make_query",
    )(low, projected, up_projection, cotangent)


def stored_at(block, half, core):
    y = block >> 4
    block_half = y >> 1
    row = jnp.where(block_half == 0, y, 3 - y)
    source = jnp.where(block_half == half, 0, 2) + jnp.where((block & 1) == core, 0, 1)
    return source * 16 + row * 8 + ((block >> 1) & 7)


def slots_of(ids_ref, me_ref, p):
    me = me_ref[0]
    core = me & 1
    half = me >> 5
    low = p >> 3
    y = jnp.where(half == 0, low, 3 - low)
    own = (y * 8 + (p & 7)) * 2 + core
    spots = [p]
    biases = [None]
    for t in (1, 2):
        block = ids_ref[own * 3 + t]
        spots.append(stored_at(block, half, core))
        biases.append(jnp.where(block == own, -jnp.inf, 0.0).astype(jnp.float32))
    return spots, biases


def attend_kernel(
    ids_ref, me_ref, qg_ref, kv0, kv1, kv2, kv3,
    out_ref, own_ref, far_ref, core_ref, farcore_ref,
    kvs, acc, staged, sem, out_sem,
):
    step = pl.program_id(0)
    flip = (me_ref[0] >> 5) * 8

    @pl.when(step == 0)
    def _():
        copies = [
            pltpu.make_async_copy(ref, kvs.at[pl.ds(16 * n, 16)], sem.at[n])
            for n, ref in enumerate((kv0, kv1, kv2, kv3))
        ]
        for copy in copies:
            copy.start()

        def clear(i, _):
            acc[i] = jnp.zeros((2, BLK, HD), jnp.float32)
            return 0

        lax.fori_loop(16, 64, clear, 0)
        for copy in copies:
            copy.wait()

    key_row = lax.broadcasted_iota(jnp.int32, (BLK, BLK), 0)
    query_col = lax.broadcasted_iota(jnp.int32, (BLK, BLK), 1)
    causal = key_row <= query_col
    work = []
    for sub in range(PER_STEP):
        spots, biases = slots_of(ids_ref, me_ref, (step * PER_STEP + sub) ^ flip)
        q = qg_ref[sub, 0]
        s = []
        for t in range(3):
            x = lax.dot_general(kvs[spots[t], 0], q, NT, preferred_element_type=jnp.float32) * LOG2_SCALE
            s.append(jnp.where(causal, x, -jnp.inf) if t == 0 else x + biases[t])
        work.append((spots, q, qg_ref[sub, 1], s))
    middle = []
    for sub, (spots, q, g, s) in enumerate(work):
        top = jnp.max(jnp.maximum(jnp.maximum(s[0], s[1]), s[2]), axis=0, keepdims=True)
        shifted = [jnp.exp2(x - top) for x in s]
        inverse = 1.0 / jnp.sum(shifted[0] + shifted[1] + shifted[2], axis=0, keepdims=True)
        probs = [x * inverse for x in shifted]
        weights = [x.astype(jnp.bfloat16) for x in probs]
        out = None
        for t in range(3):
            part = lax.dot_general(kvs[spots[t], 1], weights[t], TN, preferred_element_type=jnp.float32)
            out = part if out is None else out + part
        middle.append((probs, weights, out))
    deltas = []
    for sub, (spots, q, g, s) in enumerate(work):
        attn = middle[sub][2].T.astype(jnp.bfloat16)
        out_ref[sub, 0] = attn
        product = attn.astype(jnp.float32) * g.astype(jnp.float32)
        deltas.append(jnp.sum(product.T, axis=0, keepdims=True))

    def score_grads(sub):
        spots, _, g, _ = work[sub]
        probs = middle[sub][0]
        found = []
        for t in range(3):
            dprobs = lax.dot_general(kvs[spots[t], 1], g, NT, preferred_element_type=jnp.float32)
            found.append((probs[t] * (dprobs - deltas[sub]) * SCORE_SCALE).astype(jnp.bfloat16))
        return found

    ahead = score_grads(0)
    for sub, (spots, q, g, s) in enumerate(work):
        dscores = ahead
        if sub + 1 < PER_STEP:
            ahead = score_grads(sub + 1)
        weights = middle[sub][1]
        dq = None
        for t in range(3):
            part = lax.dot_general(kvs[spots[t], 0], dscores[t], TN, preferred_element_type=jnp.float32)
            dq = part if dq is None else dq + part
            dk = jnp.dot(dscores[t], q, preferred_element_type=jnp.float32)
            dv = jnp.dot(weights[t], g, preferred_element_type=jnp.float32)
            if t == 0:
                acc[spots[t], 0] = dk
                acc[spots[t], 1] = dv
            else:
                acc[spots[t], 0] += dk.astype(jnp.bfloat16).astype(jnp.float32)
                acc[spots[t], 1] += dv.astype(jnp.bfloat16).astype(jnp.float32)
        out_ref[sub, 1] = dq.T.astype(jnp.bfloat16)

    @pl.when(step == STEPS - 1)
    def _():
        copies = []

        def send(source, target):
            copy = pltpu.make_async_copy(source, target, out_sem.at[len(copies)])
            copy.start()
            copies.append(copy)

        send(acc.at[pl.ds(0, 16)], own_ref)
        for n, (at, target) in enumerate(((48, farcore_ref), (32, far_ref), (16, core_ref))):
            def cast(i, _, n=n, at=at):
                staged[n * 16 + i] = acc[at + i].astype(jnp.bfloat16)
                return 0
            lax.fori_loop(0, 16, cast, 0)
            send(staged.at[pl.ds(n * 16, 16)], target)
        for copy in copies:
            copy.wait()


ANY = pl.BlockSpec(memory_space=pl.ANY)


def attend(ids, me, query, key_values):
    wide = jax.ShapeDtypeStruct((16, 2, BLK, HD), jnp.float32)
    narrow = jax.ShapeDtypeStruct((16, 2, BLK, HD), jnp.bfloat16)
    rows = pl.BlockSpec(
        (PER_STEP, 2, BLK, HD), lambda i, ids_ref, me_ref: (i ^ ((me_ref[0] >> 5) * 2), 0, 0, 0)
    )
    return pl.pallas_call(
        attend_kernel,
        grid_spec=pltpu.PrefetchScalarGridSpec(
            num_scalar_prefetch=2,
            grid=(STEPS,),
            in_specs=[rows] + [ANY] * 4,
            out_specs=[rows] + [ANY] * 4,
            scratch_shapes=[
                pltpu.VMEM((64, 2, BLK, HD), jnp.bfloat16),
                pltpu.VMEM((64, 2, BLK, HD), jnp.float32),
                pltpu.VMEM((48, 2, BLK, HD), jnp.bfloat16),
                pltpu.SemaphoreType.DMA((4,)),
                pltpu.SemaphoreType.DMA((4,)),
            ],
        ),
        out_shape=[narrow, wide, narrow, narrow, narrow],
        compiler_params=pltpu.CompilerParams(vmem_limit_bytes=VMEM_BYTES),
        cost_estimate=pl.CostEstimate(
            flops=16 * 6 * 2 * BLK * 3 * BLK * HD,
            bytes_accessed=26 * 2**20,
            transcendentals=16 * 3 * BLK * BLK,
        ),
        name="attend",
    )(ids, me, query, *key_values)


def write_terms(heads, lows, ups, tok_ref, at):
    dlows = []
    for member, (head, low, up) in enumerate(zip(heads, lows, ups)):
        dlow = None
        for pair in range(HEADS // 2):
            g = jnp.concatenate([head(2 * pair), head(2 * pair + 1)], axis=1)
            part = lax.dot_general(up(pair), g, NT, preferred_element_type=jnp.float32)
            dlow = part if dlow is None else dlow + part
            up_term = jnp.dot(low, g, preferred_element_type=jnp.float32) * (ADAPTER_SCALE * GRAD_SCALE)
            for n in range(4):
                cut = up_term[:, n * 64 : (n + 1) * 64]
                ref, slot = at(member, 4 * pair + n)
                ref[slot, 32:48, :] = jnp.concatenate([cut[0:16], cut[16:32]], axis=1)
        dlows.append((dlow * ADAPTER_SCALE).astype(jnp.bfloat16))
    dlow = dlows[0] if len(dlows) == 1 else jnp.concatenate(dlows, axis=0)
    for pair in range(TILES // 2):
        rows = tok_ref[:, pair * 256 : (pair + 1) * 256]
        down_term = jnp.dot(dlow, rows, preferred_element_type=jnp.float32) * GRAD_SCALE
        for member in range(len(dlows)):
            for side in range(2):
                ref, slot = at(member, 2 * pair + side)
                ref[slot, 0:32, :] = down_term[member * R : (member + 1) * R, side * 128 : (side + 1) * 128]


def query_grads_kernel(me_ref, home_ref, tok_ref, low_ref, up_ref, attn_ref, gp_ref, keep_ref, send_ref, terms):
    me = me_ref[0]
    for h in range(HEADS):
        cols = slice(h * HD, (h + 1) * HD)
        attn_ref[:, cols] = home_ref[h, 0]
        gp_ref[:, cols] = home_ref[h, 1]

    write_terms(
        [lambda h: home_ref[h, 1]],
        [low_ref[...]],
        [lambda pair: up_ref[0, :, pair * 256 : (pair + 1) * 256]],
        tok_ref,
        lambda member, t: (terms, t),
    )

    @pl.when((me & 1) == 0)
    def _():
        keep_ref[...] = terms[:, 0:24, :]
        send_ref[...] = terms[:, 24:48, :].astype(jnp.bfloat16)

    @pl.when((me & 1) == 1)
    def _():
        keep_ref[...] = terms[:, 24:48, :]
        send_ref[...] = terms[:, 0:24, :].astype(jnp.bfloat16)


def key_value_grads_kernel(
    me_ref, _, home_ref, tok_ref, low_ref, up_ref, gp_ref, keep_ref, send_ref, terms_k, terms_v, rows, sem
):
    for side in range(2):
        for h in range(HEADS):
            rows[:, side * HQ + h * HD : side * HQ + (h + 1) * HD] = home_ref[h, side]
    copy = pltpu.make_async_copy(rows, gp_ref.at[:, pl.ds(HQ, 2 * HQ)], sem)
    copy.start()
    write_terms(
        [lambda h: home_ref[h, 0], lambda h: home_ref[h, 1]],
        [low_ref[R : 2 * R, :], low_ref[2 * R : 3 * R, :]],
        [
            lambda pair: up_ref[1, :, pair * 256 : (pair + 1) * 256],
            lambda pair: up_ref[2, :, pair * 256 : (pair + 1) * 256],
        ],
        tok_ref,
        lambda member, t: ((terms_k, terms_v)[member], t),
    )
    core = me_ref[0] & 1

    @pl.when(core == 0)
    def _():
        keep_ref[...] = terms_k[...]
        send_ref[...] = terms_v[...].astype(jnp.bfloat16)

    @pl.when(core == 1)
    def _():
        keep_ref[...] = terms_v[...]
        send_ref[...] = terms_k[...].astype(jnp.bfloat16)

    copy.wait()


def query_grads(me, home, tokens, low_t, up_projection):
    return pl.pallas_call(
        query_grads_kernel,
        grid_spec=pltpu.PrefetchScalarGridSpec(
            num_scalar_prefetch=1,
            grid=(1,),
            in_specs=[
                whole(HEADS, 2, BLK, HD),
                whole(BLK, D),
                whole(R, BLK),
                whole(1, R, HQ),
            ],
            out_specs=[whole(BLK, HQ), whole(BLK, HQ), whole(TILES, 24, 128), whole(TILES, 24, 128)],
            scratch_shapes=[pltpu.VMEM((TILES, 48, 128), jnp.float32)],
        ),
        out_shape=[
            jax.ShapeDtypeStruct((BLK, HQ), jnp.bfloat16),
            jax.ShapeDtypeStruct((BLK, 3 * HQ), jnp.bfloat16),
            jax.ShapeDtypeStruct((TILES, 24, 128), jnp.float32),
            jax.ShapeDtypeStruct((TILES, 24, 128), jnp.bfloat16),
        ],
        compiler_params=pltpu.CompilerParams(vmem_limit_bytes=24 * 1024 * 1024),
        cost_estimate=pl.CostEstimate(
            flops=2 * BLK * R * (D + 2 * HQ), bytes_accessed=8 * 2**20, transcendentals=0
        ),
        name="query_grads",
    )(me, home, tokens, low_t, up_projection)


def key_value_grads(me, grad_proj, home, tokens, low_t, up_projection):
    return pl.pallas_call(
        key_value_grads_kernel,
        grid_spec=pltpu.PrefetchScalarGridSpec(
            num_scalar_prefetch=1,
            grid=(1,),
            in_specs=[
                ANY,
                whole(HEADS, 2, BLK, HD),
                whole(BLK, D),
                whole(3 * R, BLK),
                whole(3, R, HQ),
            ],
            out_specs=[ANY, whole(TILES, 48, 128), whole(TILES, 48, 128)],
            scratch_shapes=[
                pltpu.VMEM((TILES, 48, 128), jnp.float32),
                pltpu.VMEM((TILES, 48, 128), jnp.float32),
                pltpu.VMEM((BLK, 2 * HQ), jnp.bfloat16),
                pltpu.SemaphoreType.DMA,
            ],
        ),
        out_shape=[
            jax.ShapeDtypeStruct((BLK, 3 * HQ), jnp.bfloat16),
            jax.ShapeDtypeStruct((TILES, 48, 128), jnp.float32),
            jax.ShapeDtypeStruct((TILES, 48, 128), jnp.bfloat16),
        ],
        input_output_aliases={1: 0},
        compiler_params=pltpu.CompilerParams(vmem_limit_bytes=24 * 1024 * 1024),
        cost_estimate=pl.CostEstimate(
            flops=4 * BLK * R * (D + 2 * HQ), bytes_accessed=8 * 2**20, transcendentals=0
        ),
        name="key_value_grads",
    )(me, grad_proj, home, tokens, low_t, up_projection)


def finish_kernel(lane_ref, mine_ref, other_ref, down_ref, up_ref, full, down_t, up_t):
    lane = lane_ref[0]

    def fill(first, second):
        full[0:72] = first[...]
        full[72:96] = second[48:72]
        full[96:144] = second[0:48]

    @pl.when(lane < 4)
    def _():
        fill(mine_ref, other_ref)

    @pl.when(lane >= 4)
    def _():
        fill(other_ref, mine_ref)

    for m, start in enumerate((48, 0, 96)):
        down_t[...] = full[start : start + 32, :].T
        down_ref[m] = down_t[pl.ds(lane * 16, 16), :]
        up_t[...] = full[start + 32 : start + 48, :].T
        up_ref[m, :, 0:16] = up_t[pl.ds(lane * 8, 8), :]
        up_ref[m, :, 16:32] = up_t[pl.ds(lane * 8 + 64, 8), :]


def finish(lane, mine, other):
    return pl.pallas_call(
        finish_kernel,
        grid_spec=pltpu.PrefetchScalarGridSpec(
            num_scalar_prefetch=1,
            grid=(1,),
            in_specs=[whole(72, 128), whole(72, 128)],
            out_specs=[whole(3, 16, R), whole(3, 8, R)],
            scratch_shapes=[
                pltpu.VMEM((144, 128), jnp.float32),
                pltpu.VMEM((128, R), jnp.float32),
                pltpu.VMEM((128, 16), jnp.float32),
            ],
        ),
        out_shape=[
            jax.ShapeDtypeStruct((3, 16, R), jnp.float32),
            jax.ShapeDtypeStruct((3, 8, R), jnp.float32),
        ],
        compiler_params=pltpu.CompilerParams(vmem_limit_bytes=8 * 1024 * 1024),
        name="finish",
    )(lane, mine, other)


def shards(tokens, projected, down_proj, up_projection, block_ids, cotangent):
    tokens = tokens[0]
    projected = projected[0]
    me = lax.axis_index("ctx").astype(jnp.int32)
    lane = ((me & 1) * 4 + lax.axis_index("dp")).astype(jnp.int32).reshape(1)
    me = me.reshape(1)
    ids = block_ids[0].reshape(-1)

    local, low = make_key_value(tokens, projected, jnp.transpose(down_proj, (0, 2, 1)), up_projection)
    key_value = to_heads(local)
    local = make_query(low, projected, up_projection, cotangent[0])
    low_t = low.T
    local, key_value = after(local, key_value)
    far = lax.ppermute(key_value, "ctx", TO_LATER)
    query = to_heads(local)
    out, own, far_part, core_part, farcore_part = attend(
        ids, me, query, (key_value, swap(key_value), far, swap(far))
    )

    def both_cores(keep, send):
        return (keep + swap(send).astype(jnp.float32)).astype(jnp.bfloat16)

    far_sum = far_part.astype(jnp.float32) + swap(farcore_part).astype(jnp.float32)
    returned = lax.ppermute(far_sum.astype(jnp.bfloat16), "ctx", TO_EARLIER)
    out_home = to_heads(out)
    total = own + swap(core_part).astype(jnp.float32) + returned.astype(jnp.float32)
    total, out_home = after(total.astype(jnp.bfloat16), out_home)
    total_home = to_heads(total)
    attn_rows, grad_proj, keep, send = query_grads(me, out_home, tokens, low_t, up_projection)
    pieces_q = both_cores(keep, send)
    total_home, pieces_q = after(total_home, pieces_q)
    grad_proj, keep, send = key_value_grads(me, grad_proj, total_home, tokens, low_t, up_projection)
    pieces = jnp.concatenate([both_cores(keep, send), pieces_q], axis=1)
    pieces = lax.all_to_all(pieces, "ctx", 0, 0, axis_index_groups=TILE_GROUPS, tiled=True)
    mine = jnp.sum(pieces.astype(jnp.float32), axis=0)
    others = [
        lax.ppermute(mine, "dp", [(j, (j + step) % 4) for j in range(4)]) for step in (1, 2, 3)
    ]
    mine = (mine + others[0]) + (others[1] + others[2])
    grad_down, grad_up = finish(lane, mine, swap(mine))
    return attn_rows[None], grad_proj[None], grad_down, jnp.transpose(grad_up, (0, 2, 1))


def solution(mesh):
    placed = (
        P("dp", "ctx", None),
        P("dp", "ctx", None),
        P(),
        P(),
        P("dp", None, None),
        P("dp", "ctx", None),
    )
    return jax.shard_map(
        shards,
        mesh=mesh,
        in_specs=placed,
        out_specs=(
            P("dp", "ctx", None),
            P("dp", "ctx", None),
            P(None, ("ctx", "dp"), None),
            P(None, None, ("ctx", "dp")),
        ),
        check_vma=False,
    )
```

```python
import math

import jax
import jax.numpy as jnp
from jax import lax
from jax.experimental import pallas as pl
from jax.experimental.pallas import tpu as pltpu
from jax.sharding import PartitionSpec as P

BLK = 256
HD = 128
HEADS = 16
HQ = HEADS * HD
D = 4096
R = 32
ADAPTER_SCALE = 0.5
SCORE_SCALE = HD ** -0.5
LOG2_SCALE = SCORE_SCALE * math.log2(math.e)
GRAD_SCALE = (4 * 16384) ** -0.5
VMEM_BYTES = 56 * 1024 * 1024
NT = (((1,), (1,)), ((), ()))
TN = (((0,), (0,)), ((), ()))
TILES = 32
PER_STEP = 4
STEPS = 4


def place(y, z, core):
    return (y * 8 + z) * 2 + core


def group_row(half, low):
    return low if half == 0 else 3 - low


EVERY = [(y, z, c) for y in range(4) for z in range(8) for c in range(2)]
HEAD_GROUPS = [
    [place(group_row(half, low), z, core) for low in range(2) for z in range(8)]
    for half in range(2)
    for core in range(2)
]
CORE_PAIRS = [(i, i ^ 1) for i in range(64)]
TO_LATER = [(place(y, z, c), place(3 - y, z, c)) for y, z, c in EVERY if y < 2]
TO_EARLIER = [(b, a) for a, b in TO_LATER]


def to_heads(x):
    return lax.all_to_all(x, "ctx", 0, 0, axis_index_groups=HEAD_GROUPS, tiled=True)


def swap(x):
    return lax.ppermute(x, "ctx", CORE_PAIRS)


def after(x, first):
    return lax.optimization_barrier((x, first))


def whole(*shape):
    return pl.BlockSpec(shape, lambda i, *_: (0,) * len(shape))


def add_adapter(proj, low, up):
    adapter = jnp.dot(low, up, preferred_element_type=jnp.float32)
    return (proj.astype(jnp.float32) + ADAPTER_SCALE * adapter).astype(jnp.bfloat16)


def key_value_kernel(tok_ref, down_ref, k_ref, v_ref, up_ref, out_ref, low_ref, low_s):
    @pl.when(pl.program_id(0) == 0)
    def _():
        low = lax.dot_general(
            tok_ref[...], down_ref[...].reshape(3 * R, D), NT, preferred_element_type=jnp.float32
        )
        low_s[...] = low.astype(jnp.bfloat16)
        low_ref[...] = low.astype(jnp.bfloat16)

    low = low_s[...]
    for side, ref in enumerate((k_ref, v_ref)):
        m = side + 1
        field = add_adapter(ref[...], low[:, m * R : (m + 1) * R], up_ref[m])
        for h in range(8):
            out_ref[h, side] = field[:, h * HD : (h + 1) * HD]


def make_key_value(tokens, projected, down_t, up_projection):
    return pl.pallas_call(
        key_value_kernel,
        grid=(2,),
        in_specs=[
            whole(BLK, D),
            whole(3, R, D),
            pl.BlockSpec((BLK, 1024), lambda i: (0, 2 + i)),
            pl.BlockSpec((BLK, 1024), lambda i: (0, 4 + i)),
            pl.BlockSpec((3, R, 1024), lambda i: (0, 0, i)),
        ],
        out_specs=[pl.BlockSpec((8, 2, BLK, HD), lambda i: (i, 0, 0, 0)), whole(BLK, 3 * R)],
        out_shape=[
            jax.ShapeDtypeStruct((HEADS, 2, BLK, HD), jnp.bfloat16),
            jax.ShapeDtypeStruct((BLK, 3 * R), jnp.bfloat16),
        ],
        scratch_shapes=[pltpu.VMEM((BLK, 3 * R), jnp.bfloat16)],
        compiler_params=pltpu.CompilerParams(vmem_limit_bytes=VMEM_BYTES),
        cost_estimate=pl.CostEstimate(
            flops=2 * BLK * D * 3 * R + 4 * BLK * R * HQ, bytes_accessed=7 * 2**20, transcendentals=0
        ),
        name="make_key_value",
    )(tokens, down_t, projected, projected, up_projection)


def query_kernel(low_ref, proj_ref, up_ref, cot_ref, out_ref):
    field = add_adapter(proj_ref[...], low_ref[:, 0:R], up_ref[0])
    for h in range(4):
        cols = slice(h * HD, (h + 1) * HD)
        out_ref[h, 0] = field[:, cols]
        out_ref[h, 1] = cot_ref[:, cols]


def make_query(low, projected, up_projection, cotangent):
    return pl.pallas_call(
        query_kernel,
        grid=(4,),
        in_specs=[
            whole(BLK, 3 * R),
            pl.BlockSpec((BLK, 512), lambda i: (0, i)),
            pl.BlockSpec((1, R, 512), lambda i: (0, 0, i)),
            pl.BlockSpec((BLK, 512), lambda i: (0, i)),
        ],
        out_specs=pl.BlockSpec((4, 2, BLK, HD), lambda i: (i, 0, 0, 0)),
        out_shape=jax.ShapeDtypeStruct((HEADS, 2, BLK, HD), jnp.bfloat16),
        compiler_params=pltpu.CompilerParams(vmem_limit_bytes=VMEM_BYTES),
        cost_estimate=pl.CostEstimate(
            flops=2 * BLK * R * HQ, bytes_accessed=4 * 2**20, transcendentals=0
        ),
        name="make_query",
    )(low, projected, up_projection, cotangent)


def stored_at(block, half, core):
    y = block >> 4
    block_half = y >> 1
    row = jnp.where(block_half == 0, y, 3 - y)
    source = jnp.where(block_half == half, 0, 2) + jnp.where((block & 1) == core, 0, 1)
    return source * 16 + row * 8 + ((block >> 1) & 7)


def slots_of(ids_ref, me_ref, p):
    me = me_ref[0]
    core = me & 1
    half = me >> 5
    low = p >> 3
    y = jnp.where(half == 0, low, 3 - low)
    own = (y * 8 + (p & 7)) * 2 + core
    spots = [p]
    biases = [None]
    for t in (1, 2):
        block = ids_ref[own * 3 + t]
        spots.append(stored_at(block, half, core))
        biases.append(jnp.where(block == own, -jnp.inf, 0.0).astype(jnp.float32))
    return spots, biases


def attend_kernel(
    ids_ref, me_ref, qg_ref, kv0, kv1, kv2, kv3,
    out_ref, own_ref, far_ref, core_ref, farcore_ref,
    kvs, acc, staged, sem, out_sem,
):
    step = pl.program_id(0)
    flip = (me_ref[0] >> 5) * 8

    @pl.when(step == 0)
    def _():
        copies = [
            pltpu.make_async_copy(ref, kvs.at[pl.ds(16 * n, 16)], sem.at[n])
            for n, ref in enumerate((kv0, kv1, kv2, kv3))
        ]
        for copy in copies:
            copy.start()

        def clear(i, _):
            acc[i] = jnp.zeros((2, BLK, HD), jnp.float32)
            return 0

        lax.fori_loop(16, 64, clear, 0)
        for copy in copies:
            copy.wait()

    key_row = lax.broadcasted_iota(jnp.int32, (BLK, BLK), 0)
    query_col = lax.broadcasted_iota(jnp.int32, (BLK, BLK), 1)
    causal = key_row <= query_col
    work = []
    for sub in range(PER_STEP):
        spots, biases = slots_of(ids_ref, me_ref, (step * PER_STEP + sub) ^ flip)
        q = qg_ref[sub, 0]
        s = []
        for t in range(3):
            x = lax.dot_general(kvs[spots[t], 0], q, NT, preferred_element_type=jnp.float32) * LOG2_SCALE
            s.append(jnp.where(causal, x, -jnp.inf) if t == 0 else x + biases[t])
        work.append((spots, q, qg_ref[sub, 1], s))
    middle = []
    for sub, (spots, q, g, s) in enumerate(work):
        top = jnp.max(jnp.maximum(jnp.maximum(s[0], s[1]), s[2]), axis=0, keepdims=True)
        shifted = [jnp.exp2(x - top) for x in s]
        inverse = 1.0 / jnp.sum(shifted[0] + shifted[1] + shifted[2], axis=0, keepdims=True)
        probs = [x * inverse for x in shifted]
        weights = [x.astype(jnp.bfloat16) for x in probs]
        out = None
        for t in range(3):
            part = lax.dot_general(kvs[spots[t], 1], weights[t], TN, preferred_element_type=jnp.float32)
            out = part if out is None else out + part
        middle.append((probs, weights, out))
    deltas = []
    for sub, (spots, q, g, s) in enumerate(work):
        attn = middle[sub][2].T.astype(jnp.bfloat16)
        out_ref[sub, 0] = attn
        product = attn.astype(jnp.float32) * g.astype(jnp.float32)
        deltas.append(jnp.sum(product.T, axis=0, keepdims=True))

    def score_grads(sub):
        spots, _, g, _ = work[sub]
        probs = middle[sub][0]
        found = []
        for t in range(3):
            dprobs = lax.dot_general(kvs[spots[t], 1], g, NT, preferred_element_type=jnp.float32)
            found.append((probs[t] * (dprobs - deltas[sub]) * SCORE_SCALE).astype(jnp.bfloat16))
        return found

    ahead = score_grads(0)
    for sub, (spots, q, g, s) in enumerate(work):
        dscores = ahead
        if sub + 1 < PER_STEP:
            ahead = score_grads(sub + 1)
        weights = middle[sub][1]
        dq = None
        for t in range(3):
            part = lax.dot_general(kvs[spots[t], 0], dscores[t], TN, preferred_element_type=jnp.float32)
            dq = part if dq is None else dq + part
            dk = jnp.dot(dscores[t], q, preferred_element_type=jnp.float32)
            dv = jnp.dot(weights[t], g, preferred_element_type=jnp.float32)
            if t == 0:
                acc[spots[t], 0] = dk
                acc[spots[t], 1] = dv
            else:
                acc[spots[t], 0] += dk.astype(jnp.bfloat16).astype(jnp.float32)
                acc[spots[t], 1] += dv.astype(jnp.bfloat16).astype(jnp.float32)
        out_ref[sub, 1] = dq.T.astype(jnp.bfloat16)

    @pl.when(step == STEPS - 1)
    def _():
        copies = []

        def send(source, target):
            copy = pltpu.make_async_copy(source, target, out_sem.at[len(copies)])
            copy.start()
            copies.append(copy)

        send(acc.at[pl.ds(0, 16)], own_ref)
        for n, (at, target) in enumerate(((48, farcore_ref), (32, far_ref), (16, core_ref))):
            def cast(i, _, n=n, at=at):
                staged[n * 16 + i] = acc[at + i].astype(jnp.bfloat16)
                return 0
            lax.fori_loop(0, 16, cast, 0)
            send(staged.at[pl.ds(n * 16, 16)], target)
        for copy in copies:
            copy.wait()


ANY = pl.BlockSpec(memory_space=pl.ANY)


def attend(ids, me, query, key_values):
    wide = jax.ShapeDtypeStruct((16, 2, BLK, HD), jnp.float32)
    narrow = jax.ShapeDtypeStruct((16, 2, BLK, HD), jnp.bfloat16)
    rows = pl.BlockSpec(
        (PER_STEP, 2, BLK, HD), lambda i, ids_ref, me_ref: (i ^ ((me_ref[0] >> 5) * 2), 0, 0, 0)
    )
    return pl.pallas_call(
        attend_kernel,
        grid_spec=pltpu.PrefetchScalarGridSpec(
            num_scalar_prefetch=2,
            grid=(STEPS,),
            in_specs=[rows] + [ANY] * 4,
            out_specs=[rows] + [ANY] * 4,
            scratch_shapes=[
                pltpu.VMEM((64, 2, BLK, HD), jnp.bfloat16),
                pltpu.VMEM((64, 2, BLK, HD), jnp.float32),
                pltpu.VMEM((48, 2, BLK, HD), jnp.bfloat16),
                pltpu.SemaphoreType.DMA((4,)),
                pltpu.SemaphoreType.DMA((4,)),
            ],
        ),
        out_shape=[narrow, wide, narrow, narrow, narrow],
        compiler_params=pltpu.CompilerParams(vmem_limit_bytes=VMEM_BYTES),
        cost_estimate=pl.CostEstimate(
            flops=16 * 6 * 2 * BLK * 3 * BLK * HD,
            bytes_accessed=26 * 2**20,
            transcendentals=16 * 3 * BLK * BLK,
        ),
        name="attend",
    )(ids, me, query, *key_values)


def write_terms(heads, lows, ups, tok_ref, at):
    dlows = []
    for member, (head, low, up) in enumerate(zip(heads, lows, ups)):
        dlow = None
        for pair in range(HEADS // 2):
            g = jnp.concatenate([head(2 * pair), head(2 * pair + 1)], axis=1)
            part = lax.dot_general(up(pair), g, NT, preferred_element_type=jnp.float32)
            dlow = part if dlow is None else dlow + part
            up_term = jnp.dot(low, g, preferred_element_type=jnp.float32) * (ADAPTER_SCALE * GRAD_SCALE)
            for n in range(4):
                cut = up_term[:, n * 64 : (n + 1) * 64]
                ref, slot = at(member, 4 * pair + n)
                ref[slot, 32:48, :] = jnp.concatenate([cut[0:16], cut[16:32]], axis=1)
        dlows.append((dlow * ADAPTER_SCALE).astype(jnp.bfloat16))
    dlow = dlows[0] if len(dlows) == 1 else jnp.concatenate(dlows, axis=0)
    for pair in range(TILES // 2):
        rows = tok_ref[:, pair * 256 : (pair + 1) * 256]
        down_term = jnp.dot(dlow, rows, preferred_element_type=jnp.float32) * GRAD_SCALE
        for member in range(len(dlows)):
            for side in range(2):
                ref, slot = at(member, 2 * pair + side)
                ref[slot, 0:32, :] = down_term[member * R : (member + 1) * R, side * 128 : (side + 1) * 128]


def tile_slot(me, t):
    half = t >> 4
    row = (t >> 3) if half == 0 else 3 - (t >> 3)
    return ((me >> 5) ^ half) * 16 + row * 8 + (t & 7)


def query_grads_kernel(me_ref, home_ref, tok_ref, low_ref, up_ref, attn_ref, gp_ref, keep_ref, send_ref, terms):
    me = me_ref[0]
    for h in range(HEADS):
        cols = slice(h * HD, (h + 1) * HD)
        attn_ref[:, cols] = home_ref[h, 0]
        gp_ref[:, cols] = home_ref[h, 1]

    write_terms(
        [lambda h: home_ref[h, 1]],
        [low_ref[...]],
        [lambda pair: up_ref[0, :, pair * 256 : (pair + 1) * 256]],
        tok_ref,
        lambda member, t: (terms, tile_slot(me, t)),
    )

    @pl.when((me & 1) == 0)
    def _():
        keep_ref[...] = terms[:, 0:24, :]
        send_ref[...] = terms[:, 24:48, :].astype(jnp.bfloat16)

    @pl.when((me & 1) == 1)
    def _():
        keep_ref[...] = terms[:, 24:48, :]
        send_ref[...] = terms[:, 0:24, :].astype(jnp.bfloat16)


def key_value_grads_kernel(
    me_ref, _, home_ref, tok_ref, low_ref, up_ref, gp_ref, keep_ref, send_ref, terms_k, terms_v, rows, sem
):
    for side in range(2):
        for h in range(HEADS):
            rows[:, side * HQ + h * HD : side * HQ + (h + 1) * HD] = home_ref[h, side]
    copy = pltpu.make_async_copy(rows, gp_ref.at[:, pl.ds(HQ, 2 * HQ)], sem)
    copy.start()
    write_terms(
        [lambda h: home_ref[h, 0], lambda h: home_ref[h, 1]],
        [low_ref[R : 2 * R, :], low_ref[2 * R : 3 * R, :]],
        [
            lambda pair: up_ref[1, :, pair * 256 : (pair + 1) * 256],
            lambda pair: up_ref[2, :, pair * 256 : (pair + 1) * 256],
        ],
        tok_ref,
        lambda member, t: ((terms_k, terms_v)[member], tile_slot(me_ref[0], t)),
    )
    core = me_ref[0] & 1

    @pl.when(core == 0)
    def _():
        keep_ref[...] = terms_k[...]
        send_ref[...] = terms_v[...].astype(jnp.bfloat16)

    @pl.when(core == 1)
    def _():
        keep_ref[...] = terms_v[...]
        send_ref[...] = terms_k[...].astype(jnp.bfloat16)

    copy.wait()


def query_grads(me, home, tokens, low_t, up_projection):
    return pl.pallas_call(
        query_grads_kernel,
        grid_spec=pltpu.PrefetchScalarGridSpec(
            num_scalar_prefetch=1,
            grid=(1,),
            in_specs=[
                whole(HEADS, 2, BLK, HD),
                whole(BLK, D),
                whole(R, BLK),
                whole(1, R, HQ),
            ],
            out_specs=[whole(BLK, HQ), whole(BLK, HQ), whole(TILES, 24, 128), whole(TILES, 24, 128)],
            scratch_shapes=[pltpu.VMEM((TILES, 48, 128), jnp.float32)],
        ),
        out_shape=[
            jax.ShapeDtypeStruct((BLK, HQ), jnp.bfloat16),
            jax.ShapeDtypeStruct((BLK, 3 * HQ), jnp.bfloat16),
            jax.ShapeDtypeStruct((TILES, 24, 128), jnp.float32),
            jax.ShapeDtypeStruct((TILES, 24, 128), jnp.bfloat16),
        ],
        compiler_params=pltpu.CompilerParams(vmem_limit_bytes=24 * 1024 * 1024),
        cost_estimate=pl.CostEstimate(
            flops=2 * BLK * R * (D + 2 * HQ), bytes_accessed=8 * 2**20, transcendentals=0
        ),
        name="query_grads",
    )(me, home, tokens, low_t, up_projection)


def key_value_grads(me, grad_proj, home, tokens, low_t, up_projection):
    return pl.pallas_call(
        key_value_grads_kernel,
        grid_spec=pltpu.PrefetchScalarGridSpec(
            num_scalar_prefetch=1,
            grid=(1,),
            in_specs=[
                ANY,
                whole(HEADS, 2, BLK, HD),
                whole(BLK, D),
                whole(3 * R, BLK),
                whole(3, R, HQ),
            ],
            out_specs=[ANY, whole(TILES, 48, 128), whole(TILES, 48, 128)],
            scratch_shapes=[
                pltpu.VMEM((TILES, 48, 128), jnp.float32),
                pltpu.VMEM((TILES, 48, 128), jnp.float32),
                pltpu.VMEM((BLK, 2 * HQ), jnp.bfloat16),
                pltpu.SemaphoreType.DMA,
            ],
        ),
        out_shape=[
            jax.ShapeDtypeStruct((BLK, 3 * HQ), jnp.bfloat16),
            jax.ShapeDtypeStruct((TILES, 48, 128), jnp.float32),
            jax.ShapeDtypeStruct((TILES, 48, 128), jnp.bfloat16),
        ],
        input_output_aliases={1: 0},
        compiler_params=pltpu.CompilerParams(vmem_limit_bytes=24 * 1024 * 1024),
        cost_estimate=pl.CostEstimate(
            flops=4 * BLK * R * (D + 2 * HQ), bytes_accessed=8 * 2**20, transcendentals=0
        ),
        name="key_value_grads",
    )(me, grad_proj, home, tokens, low_t, up_projection)


def finish_kernel(lane_ref, mine_ref, other_ref, down_ref, up_ref, full, down_t, up_t):
    lane = lane_ref[0]

    def fill(first, second):
        full[0:72] = first[...]
        full[72:96] = second[48:72]
        full[96:144] = second[0:48]

    @pl.when(lane < 4)
    def _():
        fill(mine_ref, other_ref)

    @pl.when(lane >= 4)
    def _():
        fill(other_ref, mine_ref)

    for m, start in enumerate((48, 0, 96)):
        down_t[...] = full[start : start + 32, :].T
        down_ref[m] = down_t[pl.ds(lane * 16, 16), :]
        up_t[...] = full[start + 32 : start + 48, :].T
        up_ref[m, :, 0:16] = up_t[pl.ds(lane * 8, 8), :]
        up_ref[m, :, 16:32] = up_t[pl.ds(lane * 8 + 64, 8), :]


def finish(lane, mine, other):
    return pl.pallas_call(
        finish_kernel,
        grid_spec=pltpu.PrefetchScalarGridSpec(
            num_scalar_prefetch=1,
            grid=(1,),
            in_specs=[whole(72, 128), whole(72, 128)],
            out_specs=[whole(3, 16, R), whole(3, 8, R)],
            scratch_shapes=[
                pltpu.VMEM((144, 128), jnp.float32),
                pltpu.VMEM((128, R), jnp.float32),
                pltpu.VMEM((128, 16), jnp.float32),
            ],
        ),
        out_shape=[
            jax.ShapeDtypeStruct((3, 16, R), jnp.float32),
            jax.ShapeDtypeStruct((3, 8, R), jnp.float32),
        ],
        compiler_params=pltpu.CompilerParams(vmem_limit_bytes=8 * 1024 * 1024),
        name="finish",
    )(lane, mine, other)


def shards(tokens, projected, down_proj, up_projection, block_ids, cotangent):
    tokens = tokens[0]
    projected = projected[0]
    me = lax.axis_index("ctx").astype(jnp.int32)
    lane = ((me & 1) * 4 + lax.axis_index("dp")).astype(jnp.int32).reshape(1)
    me = me.reshape(1)
    ids = block_ids[0].reshape(-1)

    local, low = make_key_value(tokens, projected, jnp.transpose(down_proj, (0, 2, 1)), up_projection)
    key_value = to_heads(local)
    local = make_query(low, projected, up_projection, cotangent[0])
    low_t = low.T
    local, key_value = after(local, key_value)
    far = lax.ppermute(key_value, "ctx", TO_LATER)
    query = to_heads(local)
    out, own, far_part, core_part, farcore_part = attend(
        ids, me, query, (key_value, swap(key_value), far, swap(far))
    )

    def over_cores_and_halves(keep, send):
        both = keep + swap(send).astype(jnp.float32)
        sent = lax.ppermute(both[16:].astype(jnp.bfloat16), "ctx", TO_LATER + TO_EARLIER)
        return (both[:16] + sent.astype(jnp.float32)).astype(jnp.bfloat16)

    far_sum = far_part.astype(jnp.float32) + swap(farcore_part).astype(jnp.float32)
    returned = lax.ppermute(far_sum.astype(jnp.bfloat16), "ctx", TO_EARLIER)
    out_home = to_heads(out)
    total = own + swap(core_part).astype(jnp.float32) + returned.astype(jnp.float32)
    total, out_home = after(total.astype(jnp.bfloat16), out_home)
    total_home = to_heads(total)
    attn_rows, grad_proj, keep, send = query_grads(me, out_home, tokens, low_t, up_projection)
    pieces_q = over_cores_and_halves(keep, send)
    total_home, pieces_q = after(total_home, pieces_q)
    grad_proj, keep, send = key_value_grads(me, grad_proj, total_home, tokens, low_t, up_projection)
    pieces = to_heads(jnp.concatenate([over_cores_and_halves(keep, send), pieces_q], axis=1))
    mine = jnp.sum(pieces.astype(jnp.float32), axis=0)
    others = [
        lax.ppermute(mine, "dp", [(j, (j + step) % 4) for j in range(4)]) for step in (1, 2, 3)
    ]
    mine = (mine + others[0]) + (others[1] + others[2])
    grad_down, grad_up = finish(lane, mine, swap(mine))
    return attn_rows[None], grad_proj[None], grad_down, jnp.transpose(grad_up, (0, 2, 1))


def solution(mesh):
    placed = (
        P("dp", "ctx", None),
        P("dp", "ctx", None),
        P(),
        P(),
        P("dp", None, None),
        P("dp", "ctx", None),
    )
    return jax.shard_map(
        shards,
        mesh=mesh,
        in_specs=placed,
        out_specs=(
            P("dp", "ctx", None),
            P("dp", "ctx", None),
            P(None, ("ctx", "dp"), None),
            P(None, None, ("ctx", "dp")),
        ),
        check_vma=False,
    )
```

```python
import math

import jax
import jax.numpy as jnp
from jax import lax
from jax.experimental import pallas as pl
from jax.experimental.pallas import tpu as pltpu
from jax.sharding import PartitionSpec as P

BLK = 256
HD = 128
HEADS = 16
HQ = HEADS * HD
D = 4096
R = 32
ADAPTER_SCALE = 0.5
SCORE_SCALE = HD ** -0.5
LOG2_SCALE = SCORE_SCALE * math.log2(math.e)
GRAD_SCALE = (4 * 16384) ** -0.5
VMEM_BYTES = 56 * 1024 * 1024
NT = (((1,), (1,)), ((), ()))
TN = (((0,), (0,)), ((), ()))
TILES = 32
PER_STEP = 4
STEPS = 4


def place(y, z, core):
    return (y * 8 + z) * 2 + core


def group_row(half, low):
    return low if half == 0 else 3 - low


EVERY = [(y, z, c) for y in range(4) for z in range(8) for c in range(2)]
HEAD_GROUPS = [
    [place(group_row(half, low), z, core) for low in range(2) for z in range(8)]
    for half in range(2)
    for core in range(2)
]
CORE_PAIRS = [(i, i ^ 1) for i in range(64)]
TO_LATER = [(place(y, z, c), place(3 - y, z, c)) for y, z, c in EVERY if y < 2]
TO_EARLIER = [(b, a) for a, b in TO_LATER]


def to_heads(x):
    return lax.all_to_all(x, "ctx", 0, 0, axis_index_groups=HEAD_GROUPS, tiled=True)


def swap(x):
    return lax.ppermute(x, "ctx", CORE_PAIRS)


def after(x, first):
    return lax.optimization_barrier((x, first))


def whole(*shape):
    return pl.BlockSpec(shape, lambda i, *_: (0,) * len(shape))


def add_adapter(proj, low, up):
    adapter = jnp.dot(low, up, preferred_element_type=jnp.float32)
    return (proj.astype(jnp.float32) + ADAPTER_SCALE * adapter).astype(jnp.bfloat16)


def key_value_kernel(tok_ref, down_ref, k_ref, v_ref, up_ref, out_ref, low_ref, low_s):
    @pl.when(pl.program_id(0) == 0)
    def _():
        low = lax.dot_general(
            tok_ref[...], down_ref[...].reshape(3 * R, D), NT, preferred_element_type=jnp.float32
        )
        low_s[...] = low.astype(jnp.bfloat16)
        low_ref[...] = low.astype(jnp.bfloat16)

    low = low_s[...]
    for side, ref in enumerate((k_ref, v_ref)):
        m = side + 1
        field = add_adapter(ref[...], low[:, m * R : (m + 1) * R], up_ref[m])
        for h in range(8):
            out_ref[h, side] = field[:, h * HD : (h + 1) * HD]


def make_key_value(tokens, projected, down_t, up_projection):
    return pl.pallas_call(
        key_value_kernel,
        grid=(2,),
        in_specs=[
            whole(BLK, D),
            whole(3, R, D),
            pl.BlockSpec((BLK, 1024), lambda i: (0, 2 + i)),
            pl.BlockSpec((BLK, 1024), lambda i: (0, 4 + i)),
            pl.BlockSpec((3, R, 1024), lambda i: (0, 0, i)),
        ],
        out_specs=[pl.BlockSpec((8, 2, BLK, HD), lambda i: (i, 0, 0, 0)), whole(BLK, 3 * R)],
        out_shape=[
            jax.ShapeDtypeStruct((HEADS, 2, BLK, HD), jnp.bfloat16),
            jax.ShapeDtypeStruct((BLK, 3 * R), jnp.bfloat16),
        ],
        scratch_shapes=[pltpu.VMEM((BLK, 3 * R), jnp.bfloat16)],
        compiler_params=pltpu.CompilerParams(vmem_limit_bytes=VMEM_BYTES),
        cost_estimate=pl.CostEstimate(
            flops=2 * BLK * D * 3 * R + 4 * BLK * R * HQ, bytes_accessed=7 * 2**20, transcendentals=0
        ),
        name="make_key_value",
    )(tokens, down_t, projected, projected, up_projection)


def query_kernel(low_ref, proj_ref, up_ref, cot_ref, out_ref):
    field = add_adapter(proj_ref[...], low_ref[:, 0:R], up_ref[0])
    for h in range(4):
        cols = slice(h * HD, (h + 1) * HD)
        out_ref[h, 0] = field[:, cols]
        out_ref[h, 1] = cot_ref[:, cols]


def make_query(low, projected, up_projection, cotangent):
    return pl.pallas_call(
        query_kernel,
        grid=(4,),
        in_specs=[
            whole(BLK, 3 * R),
            pl.BlockSpec((BLK, 512), lambda i: (0, i)),
            pl.BlockSpec((1, R, 512), lambda i: (0, 0, i)),
            pl.BlockSpec((BLK, 512), lambda i: (0, i)),
        ],
        out_specs=pl.BlockSpec((4, 2, BLK, HD), lambda i: (i, 0, 0, 0)),
        out_shape=jax.ShapeDtypeStruct((HEADS, 2, BLK, HD), jnp.bfloat16),
        compiler_params=pltpu.CompilerParams(vmem_limit_bytes=VMEM_BYTES),
        cost_estimate=pl.CostEstimate(
            flops=2 * BLK * R * HQ, bytes_accessed=4 * 2**20, transcendentals=0
        ),
        name="make_query",
    )(low, projected, up_projection, cotangent)


def stored_at(block, half, core):
    y = block >> 4
    block_half = y >> 1
    row = jnp.where(block_half == 0, y, 3 - y)
    source = jnp.where(block_half == half, 0, 2) + jnp.where((block & 1) == core, 0, 1)
    return source * 16 + row * 8 + ((block >> 1) & 7)


def slots_of(ids_ref, me_ref, p):
    me = me_ref[0]
    core = me & 1
    half = me >> 5
    low = p >> 3
    y = jnp.where(half == 0, low, 3 - low)
    own = (y * 8 + (p & 7)) * 2 + core
    spots = [p]
    biases = [None]
    for t in (1, 2):
        block = ids_ref[own * 3 + t]
        spots.append(stored_at(block, half, core))
        biases.append(jnp.where(block == own, -jnp.inf, 0.0).astype(jnp.float32))
    return spots, biases


def attend_kernel(
    ids_ref, me_ref, qg_ref, kv0, kv1, kv2, kv3,
    out_ref, own_ref, far_ref, core_ref, farcore_ref,
    kvs, acc, staged, sem, out_sem,
):
    step = pl.program_id(0)
    flip = (me_ref[0] >> 5) * 8

    @pl.when(step == 0)
    def _():
        copies = [
            pltpu.make_async_copy(ref, kvs.at[pl.ds(16 * n, 16)], sem.at[n])
            for n, ref in enumerate((kv0, kv1, kv2, kv3))
        ]
        for copy in copies:
            copy.start()

        def clear(i, _):
            acc[i] = jnp.zeros((2, BLK, HD), jnp.float32)
            return 0

        lax.fori_loop(16, 64, clear, 0)
        for copy in copies:
            copy.wait()

    key_row = lax.broadcasted_iota(jnp.int32, (BLK, BLK), 0)
    query_col = lax.broadcasted_iota(jnp.int32, (BLK, BLK), 1)
    causal = key_row <= query_col
    work = []
    for sub in range(PER_STEP):
        spots, biases = slots_of(ids_ref, me_ref, (step * PER_STEP + sub) ^ flip)
        q = qg_ref[sub, 0]
        s = []
        for t in range(3):
            x = lax.dot_general(kvs[spots[t], 0], q, NT, preferred_element_type=jnp.float32) * LOG2_SCALE
            s.append(jnp.where(causal, x, -jnp.inf) if t == 0 else x + biases[t])
        work.append((spots, q, qg_ref[sub, 1], s))
    middle = []
    for sub, (spots, q, g, s) in enumerate(work):
        top = jnp.max(jnp.maximum(jnp.maximum(s[0], s[1]), s[2]), axis=0, keepdims=True)
        shifted = [jnp.exp2(x - top) for x in s]
        inverse = 1.0 / jnp.sum(shifted[0] + shifted[1] + shifted[2], axis=0, keepdims=True)
        probs = [x * inverse for x in shifted]
        weights = [x.astype(jnp.bfloat16) for x in probs]
        out = None
        for t in range(3):
            part = lax.dot_general(kvs[spots[t], 1], weights[t], TN, preferred_element_type=jnp.float32)
            out = part if out is None else out + part
        middle.append((probs, weights, out))
    deltas = []
    for sub, (spots, q, g, s) in enumerate(work):
        attn = middle[sub][2].T.astype(jnp.bfloat16)
        out_ref[sub, 0] = attn
        product = attn.astype(jnp.float32) * g.astype(jnp.float32)
        deltas.append(jnp.sum(product.T, axis=0, keepdims=True))

    def score_grads(sub):
        spots, _, g, _ = work[sub]
        probs = middle[sub][0]
        found = []
        for t in range(3):
            dprobs = lax.dot_general(kvs[spots[t], 1], g, NT, preferred_element_type=jnp.float32)
            found.append((probs[t] * (dprobs - deltas[sub]) * SCORE_SCALE).astype(jnp.bfloat16))
        return found

    ahead = score_grads(0)
    for sub, (spots, q, g, s) in enumerate(work):
        dscores = ahead
        if sub + 1 < PER_STEP:
            ahead = score_grads(sub + 1)
        weights = middle[sub][1]
        dq = None
        for t in range(3):
            part = lax.dot_general(kvs[spots[t], 0], dscores[t], TN, preferred_element_type=jnp.float32)
            dq = part if dq is None else dq + part
            dk = jnp.dot(dscores[t], q, preferred_element_type=jnp.float32)
            dv = jnp.dot(weights[t], g, preferred_element_type=jnp.float32)
            if t == 0:
                acc[spots[t], 0] = dk
                acc[spots[t], 1] = dv
            else:
                acc[spots[t], 0] += dk.astype(jnp.bfloat16).astype(jnp.float32)
                acc[spots[t], 1] += dv.astype(jnp.bfloat16).astype(jnp.float32)
        out_ref[sub, 1] = dq.T.astype(jnp.bfloat16)

    @pl.when(step == STEPS - 1)
    def _():
        copies = []

        def send(source, target):
            copy = pltpu.make_async_copy(source, target, out_sem.at[len(copies)])
            copy.start()
            copies.append(copy)

        send(acc.at[pl.ds(0, 16)], own_ref)
        for n, (at, target) in enumerate(((48, farcore_ref), (32, far_ref), (16, core_ref))):
            def cast(i, _, n=n, at=at):
                staged[n * 16 + i] = acc[at + i].astype(jnp.bfloat16)
                return 0
            lax.fori_loop(0, 16, cast, 0)
            send(staged.at[pl.ds(n * 16, 16)], target)
        for copy in copies:
            copy.wait()


ANY = pl.BlockSpec(memory_space=pl.ANY)


def attend(ids, me, query, key_values):
    wide = jax.ShapeDtypeStruct((16, 2, BLK, HD), jnp.float32)
    narrow = jax.ShapeDtypeStruct((16, 2, BLK, HD), jnp.bfloat16)
    rows = pl.BlockSpec(
        (PER_STEP, 2, BLK, HD), lambda i, ids_ref, me_ref: (i ^ ((me_ref[0] >> 5) * 2), 0, 0, 0)
    )
    return pl.pallas_call(
        attend_kernel,
        grid_spec=pltpu.PrefetchScalarGridSpec(
            num_scalar_prefetch=2,
            grid=(STEPS,),
            in_specs=[rows] + [ANY] * 4,
            out_specs=[rows] + [ANY] * 4,
            scratch_shapes=[
                pltpu.VMEM((64, 2, BLK, HD), jnp.bfloat16),
                pltpu.VMEM((64, 2, BLK, HD), jnp.float32),
                pltpu.VMEM((48, 2, BLK, HD), jnp.bfloat16),
                pltpu.SemaphoreType.DMA((4,)),
                pltpu.SemaphoreType.DMA((4,)),
            ],
        ),
        out_shape=[narrow, wide, narrow, narrow, narrow],
        compiler_params=pltpu.CompilerParams(vmem_limit_bytes=VMEM_BYTES),
        cost_estimate=pl.CostEstimate(
            flops=16 * 6 * 2 * BLK * 3 * BLK * HD,
            bytes_accessed=26 * 2**20,
            transcendentals=16 * 3 * BLK * BLK,
        ),
        name="attend",
    )(ids, me, query, *key_values)


def write_terms(heads, lows, ups, tok_ref, at):
    dlows = []
    for member, (head, low, up) in enumerate(zip(heads, lows, ups)):
        dlow = None
        for pair in range(HEADS // 2):
            g = jnp.concatenate([head(2 * pair), head(2 * pair + 1)], axis=1)
            part = lax.dot_general(up(pair), g, NT, preferred_element_type=jnp.float32)
            dlow = part if dlow is None else dlow + part
            up_term = jnp.dot(low, g, preferred_element_type=jnp.float32) * (ADAPTER_SCALE * GRAD_SCALE)
            for n in range(4):
                cut = up_term[:, n * 64 : (n + 1) * 64]
                ref, slot = at(member, 4 * pair + n)
                ref[slot, 32:48, :] = jnp.concatenate([cut[0:16], cut[16:32]], axis=1)
        dlows.append((dlow * ADAPTER_SCALE).astype(jnp.bfloat16))
    dlow = dlows[0] if len(dlows) == 1 else jnp.concatenate(dlows, axis=0)
    for pair in range(TILES // 2):
        rows = tok_ref[:, pair * 256 : (pair + 1) * 256]
        down_term = jnp.dot(dlow, rows, preferred_element_type=jnp.float32) * GRAD_SCALE
        for member in range(len(dlows)):
            for side in range(2):
                ref, slot = at(member, 2 * pair + side)
                ref[slot, 0:32, :] = down_term[member * R : (member + 1) * R, side * 128 : (side + 1) * 128]


def tile_slot(me, t):
    half = t >> 4
    row = (t >> 3) if half == 0 else 3 - (t >> 3)
    return ((me >> 5) ^ half) * 16 + row * 8 + (t & 7)


def query_grads_kernel(me_ref, home_ref, tok_ref, low_ref, up_ref, attn_ref, gp_ref, keep_ref, send_ref, terms):
    me = me_ref[0]
    for h in range(HEADS):
        cols = slice(h * HD, (h + 1) * HD)
        attn_ref[:, cols] = home_ref[h, 0]
        gp_ref[:, cols] = home_ref[h, 1]

    write_terms(
        [lambda h: home_ref[h, 1]],
        [low_ref[...]],
        [lambda pair: up_ref[0, :, pair * 256 : (pair + 1) * 256]],
        tok_ref,
        lambda member, t: (terms, tile_slot(me, t)),
    )

    @pl.when((me & 1) == 0)
    def _():
        keep_ref[...] = terms[:, 0:24, :]
        send_ref[...] = terms[:, 24:48, :]

    @pl.when((me & 1) == 1)
    def _():
        keep_ref[...] = terms[:, 24:48, :]
        send_ref[...] = terms[:, 0:24, :]


def key_value_grads_kernel(
    me_ref, _, home_ref, tok_ref, low_ref, up_ref, gp_ref, keep_ref, send_ref, terms_k, terms_v, rows, sem
):
    for side in range(2):
        for h in range(HEADS):
            rows[:, side * HQ + h * HD : side * HQ + (h + 1) * HD] = home_ref[h, side]
    copy = pltpu.make_async_copy(rows, gp_ref.at[:, pl.ds(HQ, 2 * HQ)], sem)
    copy.start()
    write_terms(
        [lambda h: home_ref[h, 0], lambda h: home_ref[h, 1]],
        [low_ref[R : 2 * R, :], low_ref[2 * R : 3 * R, :]],
        [
            lambda pair: up_ref[1, :, pair * 256 : (pair + 1) * 256],
            lambda pair: up_ref[2, :, pair * 256 : (pair + 1) * 256],
        ],
        tok_ref,
        lambda member, t: ((terms_k, terms_v)[member], tile_slot(me_ref[0], t)),
    )
    core = me_ref[0] & 1

    @pl.when(core == 0)
    def _():
        keep_ref[...] = terms_k[...]
        send_ref[...] = terms_v[...].astype(jnp.bfloat16)

    @pl.when(core == 1)
    def _():
        keep_ref[...] = terms_v[...]
        send_ref[...] = terms_k[...].astype(jnp.bfloat16)

    copy.wait()


def query_grads(me, home, tokens, low_t, up_projection):
    return pl.pallas_call(
        query_grads_kernel,
        grid_spec=pltpu.PrefetchScalarGridSpec(
            num_scalar_prefetch=1,
            grid=(1,),
            in_specs=[
                whole(HEADS, 2, BLK, HD),
                whole(BLK, D),
                whole(R, BLK),
                whole(1, R, HQ),
            ],
            out_specs=[whole(BLK, HQ), whole(BLK, HQ), whole(TILES, 24, 128), whole(TILES, 24, 128)],
            scratch_shapes=[pltpu.VMEM((TILES, 48, 128), jnp.float32)],
        ),
        out_shape=[
            jax.ShapeDtypeStruct((BLK, HQ), jnp.bfloat16),
            jax.ShapeDtypeStruct((BLK, 3 * HQ), jnp.bfloat16),
            jax.ShapeDtypeStruct((TILES, 24, 128), jnp.float32),
            jax.ShapeDtypeStruct((TILES, 24, 128), jnp.float32),
        ],
        compiler_params=pltpu.CompilerParams(vmem_limit_bytes=24 * 1024 * 1024),
        cost_estimate=pl.CostEstimate(
            flops=2 * BLK * R * (D + 2 * HQ), bytes_accessed=8 * 2**20, transcendentals=0
        ),
        name="query_grads",
    )(me, home, tokens, low_t, up_projection)


def key_value_grads(me, grad_proj, home, tokens, low_t, up_projection):
    return pl.pallas_call(
        key_value_grads_kernel,
        grid_spec=pltpu.PrefetchScalarGridSpec(
            num_scalar_prefetch=1,
            grid=(1,),
            in_specs=[
                ANY,
                whole(HEADS, 2, BLK, HD),
                whole(BLK, D),
                whole(3 * R, BLK),
                whole(3, R, HQ),
            ],
            out_specs=[ANY, whole(TILES, 48, 128), whole(TILES, 48, 128)],
            scratch_shapes=[
                pltpu.VMEM((TILES, 48, 128), jnp.float32),
                pltpu.VMEM((TILES, 48, 128), jnp.float32),
                pltpu.VMEM((BLK, 2 * HQ), jnp.bfloat16),
                pltpu.SemaphoreType.DMA,
            ],
        ),
        out_shape=[
            jax.ShapeDtypeStruct((BLK, 3 * HQ), jnp.bfloat16),
            jax.ShapeDtypeStruct((TILES, 48, 128), jnp.float32),
            jax.ShapeDtypeStruct((TILES, 48, 128), jnp.bfloat16),
        ],
        input_output_aliases={1: 0},
        compiler_params=pltpu.CompilerParams(vmem_limit_bytes=24 * 1024 * 1024),
        cost_estimate=pl.CostEstimate(
            flops=4 * BLK * R * (D + 2 * HQ), bytes_accessed=8 * 2**20, transcendentals=0
        ),
        name="key_value_grads",
    )(me, grad_proj, home, tokens, low_t, up_projection)


def finish_kernel(lane_ref, mine_ref, other_ref, down_ref, up_ref, full, down_t, up_t):
    lane = lane_ref[0]

    def fill(first, second):
        full[0:72] = first[...]
        full[72:96] = second[48:72]
        full[96:144] = second[0:48]

    @pl.when(lane < 4)
    def _():
        fill(mine_ref, other_ref)

    @pl.when(lane >= 4)
    def _():
        fill(other_ref, mine_ref)

    for m, start in enumerate((48, 0, 96)):
        down_t[...] = full[start : start + 32, :].T
        down_ref[m] = down_t[pl.ds(lane * 16, 16), :]
        up_t[...] = full[start + 32 : start + 48, :].T
        up_ref[m, :, 0:16] = up_t[pl.ds(lane * 8, 8), :]
        up_ref[m, :, 16:32] = up_t[pl.ds(lane * 8 + 64, 8), :]


def finish(lane, mine, other):
    return pl.pallas_call(
        finish_kernel,
        grid_spec=pltpu.PrefetchScalarGridSpec(
            num_scalar_prefetch=1,
            grid=(1,),
            in_specs=[whole(72, 128), whole(72, 128)],
            out_specs=[whole(3, 16, R), whole(3, 8, R)],
            scratch_shapes=[
                pltpu.VMEM((144, 128), jnp.float32),
                pltpu.VMEM((128, R), jnp.float32),
                pltpu.VMEM((128, 16), jnp.float32),
            ],
        ),
        out_shape=[
            jax.ShapeDtypeStruct((3, 16, R), jnp.float32),
            jax.ShapeDtypeStruct((3, 8, R), jnp.float32),
        ],
        compiler_params=pltpu.CompilerParams(vmem_limit_bytes=8 * 1024 * 1024),
        name="finish",
    )(lane, mine, other)


def shards(tokens, projected, down_proj, up_projection, block_ids, cotangent):
    tokens = tokens[0]
    projected = projected[0]
    me = lax.axis_index("ctx").astype(jnp.int32)
    lane = ((me & 1) * 4 + lax.axis_index("dp")).astype(jnp.int32).reshape(1)
    me = me.reshape(1)
    ids = block_ids[0].reshape(-1)

    local, low = make_key_value(tokens, projected, jnp.transpose(down_proj, (0, 2, 1)), up_projection)
    key_value = to_heads(local)
    local = make_query(low, projected, up_projection, cotangent[0])
    low_t = low.T
    local, key_value = after(local, key_value)
    far = lax.ppermute(key_value, "ctx", TO_LATER)
    query = to_heads(local)
    out, own, far_part, core_part, farcore_part = attend(
        ids, me, query, (key_value, swap(key_value), far, swap(far))
    )

    def over_cores_and_halves(keep, send):
        both = keep + swap(send).astype(jnp.float32)
        sent = lax.ppermute(both[16:].astype(jnp.bfloat16), "ctx", TO_LATER + TO_EARLIER)
        return (both[:16] + sent.astype(jnp.float32)).astype(jnp.bfloat16)

    far_sum = far_part.astype(jnp.float32) + swap(farcore_part).astype(jnp.float32)
    returned = lax.ppermute(far_sum.astype(jnp.bfloat16), "ctx", TO_EARLIER)
    out_home = to_heads(out)
    total = own + swap(core_part).astype(jnp.float32) + returned.astype(jnp.float32)
    total, out_home = after(total.astype(jnp.bfloat16), out_home)
    total_home = to_heads(total)
    attn_rows, grad_proj, keep, send = query_grads(me, out_home, tokens, low_t, up_projection)
    pieces_q = over_cores_and_halves(keep, send)
    total_home, pieces_q = after(total_home, pieces_q)
    grad_proj, keep, send = key_value_grads(me, grad_proj, total_home, tokens, low_t, up_projection)
    pieces = to_heads(jnp.concatenate([over_cores_and_halves(keep, send), pieces_q], axis=1))
    mine = jnp.sum(pieces.astype(jnp.float32), axis=0)
    others = [
        lax.ppermute(mine, "dp", [(j, (j + step) % 4) for j in range(4)]) for step in (1, 2, 3)
    ]
    mine = (mine + others[0]) + (others[1] + others[2])
    grad_down, grad_up = finish(lane, mine, swap(mine))
    return attn_rows[None], grad_proj[None], grad_down, jnp.transpose(grad_up, (0, 2, 1))


def solution(mesh):
    placed = (
        P("dp", "ctx", None),
        P("dp", "ctx", None),
        P(),
        P(),
        P("dp", None, None),
        P("dp", "ctx", None),
    )
    return jax.shard_map(
        shards,
        mesh=mesh,
        in_specs=placed,
        out_specs=(
            P("dp", "ctx", None),
            P("dp", "ctx", None),
            P(None, ("ctx", "dp"), None),
            P(None, None, ("ctx", "dp")),
        ),
        check_vma=False,
    )
```

```python
import math

import jax
import jax.numpy as jnp
from jax import lax
from jax.experimental import pallas as pl
from jax.experimental.pallas import tpu as pltpu
from jax.sharding import PartitionSpec as P

BLK = 256
HD = 128
HEADS = 16
HQ = HEADS * HD
D = 4096
R = 32
ADAPTER_SCALE = 0.5
SCORE_SCALE = HD ** -0.5
LOG2_SCALE = SCORE_SCALE * math.log2(math.e)
GRAD_SCALE = (4 * 16384) ** -0.5
VMEM_BYTES = 56 * 1024 * 1024
NT = (((1,), (1,)), ((), ()))
TN = (((0,), (0,)), ((), ()))
TILES = 32
PER_STEP = 4
STEPS = 4


def place(y, z, core):
    return (y * 8 + z) * 2 + core


def group_row(half, low):
    return low if half == 0 else 3 - low


EVERY = [(y, z, c) for y in range(4) for z in range(8) for c in range(2)]
HEAD_GROUPS = [
    [place(group_row(half, low), z, core) for low in range(2) for z in range(8)]
    for half in range(2)
    for core in range(2)
]
CORE_PAIRS = [(i, i ^ 1) for i in range(64)]
TO_LATER = [(place(y, z, c), place(3 - y, z, c)) for y, z, c in EVERY if y < 2]
TO_EARLIER = [(b, a) for a, b in TO_LATER]


def to_heads(x):
    return lax.all_to_all(x, "ctx", 0, 0, axis_index_groups=HEAD_GROUPS, tiled=True)


def swap(x):
    return lax.ppermute(x, "ctx", CORE_PAIRS)


def after(x, first):
    return lax.optimization_barrier((x, first))


def whole(*shape):
    return pl.BlockSpec(shape, lambda i, *_: (0,) * len(shape))


def add_adapter(proj, low, up):
    adapter = jnp.dot(low, up, preferred_element_type=jnp.float32)
    return (proj.astype(jnp.float32) + ADAPTER_SCALE * adapter).astype(jnp.bfloat16)


def key_value_kernel(tok_ref, down_ref, k_ref, v_ref, up_ref, out_ref, low_ref, low_s):
    @pl.when(pl.program_id(0) == 0)
    def _():
        low = lax.dot_general(
            tok_ref[...], down_ref[...].reshape(3 * R, D), NT, preferred_element_type=jnp.float32
        )
        low_s[...] = low.astype(jnp.bfloat16)
        low_ref[...] = low.astype(jnp.bfloat16)

    low = low_s[...]
    for side, ref in enumerate((k_ref, v_ref)):
        m = side + 1
        field = add_adapter(ref[...], low[:, m * R : (m + 1) * R], up_ref[m])
        for h in range(8):
            out_ref[h, side] = field[:, h * HD : (h + 1) * HD]


def make_key_value(tokens, projected, down_t, up_projection):
    return pl.pallas_call(
        key_value_kernel,
        grid=(2,),
        in_specs=[
            whole(BLK, D),
            whole(3, R, D),
            pl.BlockSpec((BLK, 1024), lambda i: (0, 2 + i)),
            pl.BlockSpec((BLK, 1024), lambda i: (0, 4 + i)),
            pl.BlockSpec((3, R, 1024), lambda i: (0, 0, i)),
        ],
        out_specs=[pl.BlockSpec((8, 2, BLK, HD), lambda i: (i, 0, 0, 0)), whole(BLK, 3 * R)],
        out_shape=[
            jax.ShapeDtypeStruct((HEADS, 2, BLK, HD), jnp.bfloat16),
            jax.ShapeDtypeStruct((BLK, 3 * R), jnp.bfloat16),
        ],
        scratch_shapes=[pltpu.VMEM((BLK, 3 * R), jnp.bfloat16)],
        compiler_params=pltpu.CompilerParams(vmem_limit_bytes=VMEM_BYTES),
        cost_estimate=pl.CostEstimate(
            flops=2 * BLK * D * 3 * R + 4 * BLK * R * HQ, bytes_accessed=7 * 2**20, transcendentals=0
        ),
        name="make_key_value",
    )(tokens, down_t, projected, projected, up_projection)


def query_kernel(low_ref, proj_ref, up_ref, cot_ref, out_ref):
    field = add_adapter(proj_ref[...], low_ref[:, 0:R], up_ref[0])
    for h in range(4):
        cols = slice(h * HD, (h + 1) * HD)
        out_ref[h, 0] = field[:, cols]
        out_ref[h, 1] = cot_ref[:, cols]


def make_query(low, projected, up_projection, cotangent):
    return pl.pallas_call(
        query_kernel,
        grid=(4,),
        in_specs=[
            whole(BLK, 3 * R),
            pl.BlockSpec((BLK, 512), lambda i: (0, i)),
            pl.BlockSpec((1, R, 512), lambda i: (0, 0, i)),
            pl.BlockSpec((BLK, 512), lambda i: (0, i)),
        ],
        out_specs=pl.BlockSpec((4, 2, BLK, HD), lambda i: (i, 0, 0, 0)),
        out_shape=jax.ShapeDtypeStruct((HEADS, 2, BLK, HD), jnp.bfloat16),
        compiler_params=pltpu.CompilerParams(vmem_limit_bytes=VMEM_BYTES),
        cost_estimate=pl.CostEstimate(
            flops=2 * BLK * R * HQ, bytes_accessed=4 * 2**20, transcendentals=0
        ),
        name="make_query",
    )(low, projected, up_projection, cotangent)


def stored_at(block, half, core):
    y = block >> 4
    block_half = y >> 1
    row = jnp.where(block_half == 0, y, 3 - y)
    source = jnp.where(block_half == half, 0, 2) + jnp.where((block & 1) == core, 0, 1)
    return source * 16 + row * 8 + ((block >> 1) & 7)


def slots_of(ids_ref, me_ref, p):
    me = me_ref[0]
    core = me & 1
    half = me >> 5
    low = p >> 3
    y = jnp.where(half == 0, low, 3 - low)
    own = (y * 8 + (p & 7)) * 2 + core
    spots = [p]
    biases = [None]
    for t in (1, 2):
        block = ids_ref[own * 3 + t]
        spots.append(stored_at(block, half, core))
        biases.append(jnp.where(block == own, -jnp.inf, 0.0).astype(jnp.float32))
    return spots, biases


def attend_kernel(
    ids_ref, me_ref, qg_ref, kv0, kv1, kv2, kv3,
    out_ref, own_ref, far_ref, core_ref, farcore_ref,
    kvs, acc, staged, sem, out_sem,
):
    step = pl.program_id(0)
    flip = (me_ref[0] >> 5) * 8

    @pl.when(step == 0)
    def _():
        copies = [
            pltpu.make_async_copy(ref, kvs.at[pl.ds(16 * n, 16)], sem.at[n])
            for n, ref in enumerate((kv0, kv1, kv2, kv3))
        ]
        for copy in copies:
            copy.start()

        def clear(i, _):
            acc[i] = jnp.zeros((2, BLK, HD), jnp.float32)
            return 0

        lax.fori_loop(16, 64, clear, 0)
        for copy in copies:
            copy.wait()

    key_row = lax.broadcasted_iota(jnp.int32, (BLK, BLK), 0)
    query_col = lax.broadcasted_iota(jnp.int32, (BLK, BLK), 1)
    causal = key_row <= query_col
    work = []
    for sub in range(PER_STEP):
        spots, biases = slots_of(ids_ref, me_ref, (step * PER_STEP + sub) ^ flip)
        q = qg_ref[sub, 0]
        s = []
        for t in range(3):
            x = lax.dot_general(kvs[spots[t], 0], q, NT, preferred_element_type=jnp.float32) * LOG2_SCALE
            s.append(jnp.where(causal, x, -jnp.inf) if t == 0 else x + biases[t])
        work.append((spots, q, qg_ref[sub, 1], s))
    middle = []
    for sub, (spots, q, g, s) in enumerate(work):
        top = jnp.max(jnp.maximum(jnp.maximum(s[0], s[1]), s[2]), axis=0, keepdims=True)
        shifted = [jnp.exp2(x - top) for x in s]
        inverse = 1.0 / jnp.sum(shifted[0] + shifted[1] + shifted[2], axis=0, keepdims=True)
        probs = [x * inverse for x in shifted]
        weights = [x.astype(jnp.bfloat16) for x in probs]
        out = None
        for t in range(3):
            part = lax.dot_general(kvs[spots[t], 1], weights[t], TN, preferred_element_type=jnp.float32)
            out = part if out is None else out + part
        middle.append((probs, weights, out))
    deltas = []
    for sub, (spots, q, g, s) in enumerate(work):
        attn = middle[sub][2].T.astype(jnp.bfloat16)
        out_ref[sub, 0] = attn
        product = attn.astype(jnp.float32) * g.astype(jnp.float32)
        deltas.append(jnp.sum(product.T, axis=0, keepdims=True))

    def score_grads(sub):
        spots, _, g, _ = work[sub]
        probs = middle[sub][0]
        found = []
        for t in range(3):
            dprobs = lax.dot_general(kvs[spots[t], 1], g, NT, preferred_element_type=jnp.float32)
            found.append((probs[t] * (dprobs - deltas[sub]) * SCORE_SCALE).astype(jnp.bfloat16))
        return found

    ahead = score_grads(0)
    for sub, (spots, q, g, s) in enumerate(work):
        dscores = ahead
        if sub + 1 < PER_STEP:
            ahead = score_grads(sub + 1)
        weights = middle[sub][1]
        dq = None
        for t in range(3):
            part = lax.dot_general(kvs[spots[t], 0], dscores[t], TN, preferred_element_type=jnp.float32)
            dq = part if dq is None else dq + part
            dk = jnp.dot(dscores[t], q, preferred_element_type=jnp.float32)
            dv = jnp.dot(weights[t], g, preferred_element_type=jnp.float32)
            if t == 0:
                acc[spots[t], 0] = dk
                acc[spots[t], 1] = dv
            else:
                acc[spots[t], 0] += dk.astype(jnp.bfloat16).astype(jnp.float32)
                acc[spots[t], 1] += dv.astype(jnp.bfloat16).astype(jnp.float32)
        out_ref[sub, 1] = dq.T.astype(jnp.bfloat16)

    @pl.when(step == STEPS - 1)
    def _():
        copies = []

        def send(source, target):
            copy = pltpu.make_async_copy(source, target, out_sem.at[len(copies)])
            copy.start()
            copies.append(copy)

        for n, (at, target) in enumerate(((48, farcore_ref), (32, far_ref), (0, own_ref), (16, core_ref))):
            def cast(i, _, n=n, at=at):
                staged[n * 16 + i] = acc[at + i].astype(jnp.bfloat16)
                return 0
            lax.fori_loop(0, 16, cast, 0)
            send(staged.at[pl.ds(n * 16, 16)], target)
        for copy in copies:
            copy.wait()


ANY = pl.BlockSpec(memory_space=pl.ANY)


def attend(ids, me, query, key_values):
    narrow = jax.ShapeDtypeStruct((16, 2, BLK, HD), jnp.bfloat16)
    rows = pl.BlockSpec(
        (PER_STEP, 2, BLK, HD), lambda i, ids_ref, me_ref: (i ^ ((me_ref[0] >> 5) * 2), 0, 0, 0)
    )
    return pl.pallas_call(
        attend_kernel,
        grid_spec=pltpu.PrefetchScalarGridSpec(
            num_scalar_prefetch=2,
            grid=(STEPS,),
            in_specs=[rows] + [ANY] * 4,
            out_specs=[rows] + [ANY] * 4,
            scratch_shapes=[
                pltpu.VMEM((64, 2, BLK, HD), jnp.bfloat16),
                pltpu.VMEM((64, 2, BLK, HD), jnp.float32),
                pltpu.VMEM((64, 2, BLK, HD), jnp.bfloat16),
                pltpu.SemaphoreType.DMA((4,)),
                pltpu.SemaphoreType.DMA((4,)),
            ],
        ),
        out_shape=[narrow] * 5,
        compiler_params=pltpu.CompilerParams(vmem_limit_bytes=VMEM_BYTES),
        cost_estimate=pl.CostEstimate(
            flops=16 * 6 * 2 * BLK * 3 * BLK * HD,
            bytes_accessed=26 * 2**20,
            transcendentals=16 * 3 * BLK * BLK,
        ),
        name="attend",
    )(ids, me, query, *key_values)


def write_terms(heads, lows, ups, tok_ref, at):
    dlows = []
    for member, (head, low, up) in enumerate(zip(heads, lows, ups)):
        dlow = None
        for pair in range(HEADS // 2):
            g = jnp.concatenate([head(2 * pair), head(2 * pair + 1)], axis=1)
            part = lax.dot_general(up(pair), g, NT, preferred_element_type=jnp.float32)
            dlow = part if dlow is None else dlow + part
            up_term = jnp.dot(low, g, preferred_element_type=jnp.float32) * (ADAPTER_SCALE * GRAD_SCALE)
            for n in range(4):
                cut = up_term[:, n * 64 : (n + 1) * 64]
                ref, slot = at(member, 4 * pair + n)
                ref[slot, 32:48, :] = jnp.concatenate([cut[0:16], cut[16:32]], axis=1)
        dlows.append((dlow * ADAPTER_SCALE).astype(jnp.bfloat16))
    dlow = dlows[0] if len(dlows) == 1 else jnp.concatenate(dlows, axis=0)
    for pair in range(TILES // 2):
        rows = tok_ref[:, pair * 256 : (pair + 1) * 256]
        down_term = jnp.dot(dlow, rows, preferred_element_type=jnp.float32) * GRAD_SCALE
        for member in range(len(dlows)):
            for side in range(2):
                ref, slot = at(member, 2 * pair + side)
                ref[slot, 0:32, :] = down_term[member * R : (member + 1) * R, side * 128 : (side + 1) * 128]


def tile_slot(me, t):
    half = t >> 4
    row = (t >> 3) if half == 0 else 3 - (t >> 3)
    return ((me >> 5) ^ half) * 16 + row * 8 + (t & 7)


def query_grads_kernel(me_ref, home_ref, tok_ref, low_ref, up_ref, attn_ref, gp_ref, keep_ref, send_ref, terms):
    me = me_ref[0]
    for h in range(HEADS):
        cols = slice(h * HD, (h + 1) * HD)
        attn_ref[:, cols] = home_ref[h, 0]
        gp_ref[:, cols] = home_ref[h, 1]

    write_terms(
        [lambda h: home_ref[h, 1]],
        [low_ref[...]],
        [lambda pair: up_ref[0, :, pair * 256 : (pair + 1) * 256]],
        tok_ref,
        lambda member, t: (terms, tile_slot(me, t)),
    )

    @pl.when((me & 1) == 0)
    def _():
        keep_ref[...] = terms[:, 0:24, :]
        send_ref[...] = terms[:, 24:48, :]

    @pl.when((me & 1) == 1)
    def _():
        keep_ref[...] = terms[:, 24:48, :]
        send_ref[...] = terms[:, 0:24, :]


def key_value_grads_kernel(
    me_ref, _, home_ref, tok_ref, low_ref, up_ref, gp_ref, keep_ref, send_ref, terms_k, terms_v, rows, sem
):
    for side in range(2):
        for h in range(HEADS):
            rows[:, side * HQ + h * HD : side * HQ + (h + 1) * HD] = home_ref[h, side]
    copy = pltpu.make_async_copy(rows, gp_ref.at[:, pl.ds(HQ, 2 * HQ)], sem)
    copy.start()
    write_terms(
        [lambda h: home_ref[h, 0], lambda h: home_ref[h, 1]],
        [low_ref[R : 2 * R, :], low_ref[2 * R : 3 * R, :]],
        [
            lambda pair: up_ref[1, :, pair * 256 : (pair + 1) * 256],
            lambda pair: up_ref[2, :, pair * 256 : (pair + 1) * 256],
        ],
        tok_ref,
        lambda member, t: ((terms_k, terms_v)[member], tile_slot(me_ref[0], t)),
    )
    core = me_ref[0] & 1

    @pl.when(core == 0)
    def _():
        keep_ref[...] = terms_k[...]
        send_ref[...] = terms_v[...].astype(jnp.bfloat16)

    @pl.when(core == 1)
    def _():
        keep_ref[...] = terms_v[...]
        send_ref[...] = terms_k[...].astype(jnp.bfloat16)

    copy.wait()


def query_grads(me, home, tokens, low_t, up_projection):
    return pl.pallas_call(
        query_grads_kernel,
        grid_spec=pltpu.PrefetchScalarGridSpec(
            num_scalar_prefetch=1,
            grid=(1,),
            in_specs=[
                whole(HEADS, 2, BLK, HD),
                whole(BLK, D),
                whole(R, BLK),
                whole(1, R, HQ),
            ],
            out_specs=[whole(BLK, HQ), whole(BLK, HQ), whole(TILES, 24, 128), whole(TILES, 24, 128)],
            scratch_shapes=[pltpu.VMEM((TILES, 48, 128), jnp.float32)],
        ),
        out_shape=[
            jax.ShapeDtypeStruct((BLK, HQ), jnp.bfloat16),
            jax.ShapeDtypeStruct((BLK, 3 * HQ), jnp.bfloat16),
            jax.ShapeDtypeStruct((TILES, 24, 128), jnp.float32),
            jax.ShapeDtypeStruct((TILES, 24, 128), jnp.float32),
        ],
        compiler_params=pltpu.CompilerParams(vmem_limit_bytes=24 * 1024 * 1024),
        cost_estimate=pl.CostEstimate(
            flops=2 * BLK * R * (D + 2 * HQ), bytes_accessed=8 * 2**20, transcendentals=0
        ),
        name="query_grads",
    )(me, home, tokens, low_t, up_projection)


def key_value_grads(me, grad_proj, home, tokens, low_t, up_projection):
    return pl.pallas_call(
        key_value_grads_kernel,
        grid_spec=pltpu.PrefetchScalarGridSpec(
            num_scalar_prefetch=1,
            grid=(1,),
            in_specs=[
                ANY,
                whole(HEADS, 2, BLK, HD),
                whole(BLK, D),
                whole(3 * R, BLK),
                whole(3, R, HQ),
            ],
            out_specs=[ANY, whole(TILES, 48, 128), whole(TILES, 48, 128)],
            scratch_shapes=[
                pltpu.VMEM((TILES, 48, 128), jnp.float32),
                pltpu.VMEM((TILES, 48, 128), jnp.float32),
                pltpu.VMEM((BLK, 2 * HQ), jnp.bfloat16),
                pltpu.SemaphoreType.DMA,
            ],
        ),
        out_shape=[
            jax.ShapeDtypeStruct((BLK, 3 * HQ), jnp.bfloat16),
            jax.ShapeDtypeStruct((TILES, 48, 128), jnp.float32),
            jax.ShapeDtypeStruct((TILES, 48, 128), jnp.bfloat16),
        ],
        input_output_aliases={1: 0},
        compiler_params=pltpu.CompilerParams(vmem_limit_bytes=24 * 1024 * 1024),
        cost_estimate=pl.CostEstimate(
            flops=4 * BLK * R * (D + 2 * HQ), bytes_accessed=8 * 2**20, transcendentals=0
        ),
        name="key_value_grads",
    )(me, grad_proj, home, tokens, low_t, up_projection)


def finish_kernel(lane_ref, mine_ref, other_ref, down_ref, up_ref, full, down_t, up_t):
    lane = lane_ref[0]

    def fill(first, second):
        full[0:72] = first[...]
        full[72:96] = second[48:72]
        full[96:144] = second[0:48]

    @pl.when(lane < 4)
    def _():
        fill(mine_ref, other_ref)

    @pl.when(lane >= 4)
    def _():
        fill(other_ref, mine_ref)

    for m, start in enumerate((48, 0, 96)):
        down_t[...] = full[start : start + 32, :].T
        down_ref[m] = down_t[pl.ds(lane * 16, 16), :]
        up_t[...] = full[start + 32 : start + 48, :].T
        up_ref[m, :, 0:16] = up_t[pl.ds(lane * 8, 8), :]
        up_ref[m, :, 16:32] = up_t[pl.ds(lane * 8 + 64, 8), :]


def finish(lane, mine, other):
    return pl.pallas_call(
        finish_kernel,
        grid_spec=pltpu.PrefetchScalarGridSpec(
            num_scalar_prefetch=1,
            grid=(1,),
            in_specs=[whole(72, 128), whole(72, 128)],
            out_specs=[whole(3, 16, R), whole(3, 8, R)],
            scratch_shapes=[
                pltpu.VMEM((144, 128), jnp.float32),
                pltpu.VMEM((128, R), jnp.float32),
                pltpu.VMEM((128, 16), jnp.float32),
            ],
        ),
        out_shape=[
            jax.ShapeDtypeStruct((3, 16, R), jnp.float32),
            jax.ShapeDtypeStruct((3, 8, R), jnp.float32),
        ],
        compiler_params=pltpu.CompilerParams(vmem_limit_bytes=8 * 1024 * 1024),
        name="finish",
    )(lane, mine, other)


def shards(tokens, projected, down_proj, up_projection, block_ids, cotangent):
    tokens = tokens[0]
    projected = projected[0]
    me = lax.axis_index("ctx").astype(jnp.int32)
    lane = ((me & 1) * 4 + lax.axis_index("dp")).astype(jnp.int32).reshape(1)
    me = me.reshape(1)
    ids = block_ids[0].reshape(-1)

    local, low = make_key_value(tokens, projected, jnp.transpose(down_proj, (0, 2, 1)), up_projection)
    key_value = to_heads(local)
    local = make_query(low, projected, up_projection, cotangent[0])
    low_t = low.T
    local, key_value = after(local, key_value)
    far = lax.ppermute(key_value, "ctx", TO_LATER)
    query = to_heads(local)
    out, own, far_part, core_part, farcore_part = attend(
        ids, me, query, (key_value, swap(key_value), far, swap(far))
    )

    def over_cores_and_halves(keep, send):
        both = keep + swap(send).astype(jnp.float32)
        sent = lax.ppermute(both[16:].astype(jnp.bfloat16), "ctx", TO_LATER + TO_EARLIER)
        return (both[:16] + sent.astype(jnp.float32)).astype(jnp.bfloat16)

    far_sum = far_part.astype(jnp.float32) + swap(farcore_part).astype(jnp.float32)
    returned = lax.ppermute(far_sum.astype(jnp.bfloat16), "ctx", TO_EARLIER)
    out_home = to_heads(out)
    total = own.astype(jnp.float32) + swap(core_part).astype(jnp.float32) + returned.astype(jnp.float32)
    total, out_home = after(total.astype(jnp.bfloat16), out_home)
    total_home = to_heads(total)
    attn_rows, grad_proj, keep, send = query_grads(me, out_home, tokens, low_t, up_projection)
    pieces_q = over_cores_and_halves(keep, send)
    total_home, pieces_q = after(total_home, pieces_q)
    grad_proj, keep, send = key_value_grads(me, grad_proj, total_home, tokens, low_t, up_projection)
    pieces = to_heads(jnp.concatenate([over_cores_and_halves(keep, send), pieces_q], axis=1))
    mine = jnp.sum(pieces.astype(jnp.float32), axis=0)
    others = [
        lax.ppermute(mine, "dp", [(j, (j + step) % 4) for j in range(4)]) for step in (1, 2, 3)
    ]
    mine = (mine + others[0]) + (others[1] + others[2])
    grad_down, grad_up = finish(lane, mine, swap(mine))
    return attn_rows[None], grad_proj[None], grad_down, jnp.transpose(grad_up, (0, 2, 1))


def solution(mesh):
    placed = (
        P("dp", "ctx", None),
        P("dp", "ctx", None),
        P(),
        P(),
        P("dp", None, None),
        P("dp", "ctx", None),
    )
    return jax.shard_map(
        shards,
        mesh=mesh,
        in_specs=placed,
        out_specs=(
            P("dp", "ctx", None),
            P("dp", "ctx", None),
            P(None, ("ctx", "dp"), None),
            P(None, None, ("ctx", "dp")),
        ),
        check_vma=False,
    )
```
